128 devices in a mesh: seq: 16 (over z, y), ep: 8 (over x, core).
Axes of the slice: x: 4, y: 4, z: 4, core: 2. Of those that a mesh axis runs over, the one named last changes fastest.
Arguments:
- queries: bfloat16 [4096, 4096], P('seq', 'ep'), may hold values from -6 to 6
- key_rows: bfloat16 [4096, 4096], P('seq', 'ep'), may hold values from -6 to 6
- values: bfloat16 [4096, 4096], P('seq', 'ep'), may hold values from -6 to 6
- log_decay: float32 [32, 4096], P('ep', 'seq'), may hold values from -1.5 to 0
- residual: bfloat16 [4096, 6144], P('seq', 'ep'), may hold values from -110 to 110
- w_out: bfloat16 [4096, 6144], P('ep', 'seq'), may hold values from -0.09375 to 0.09375
- w_gate: bfloat16 [8, 6144, 9216], P('ep', None, 'seq'), may hold values from -0.078125 to 0.078125
- w_up: bfloat16 [8, 6144, 9216], P('ep', None, 'seq'), may hold values from -0.078125 to 0.078125
- w_down: bfloat16 [8, 9216, 6144], P('ep', 'seq'), may hold values from -0.0625 to 0.0625
- routes: int32 [4096, 2], P('seq'), may hold values from 0 to 7, all different within a row; in each aligned block of 256 rows (0 to 255, 256 to 511, ...) at most 72 rows name the same one
- gate_values: float32 [4096, 2], P('seq'), may hold values from 0.1 to 1
Outputs:
- attention: bfloat16 [4096, 4096], P('seq', 'ep')
- expert_mix: bfloat16 [4096, 6144], P('seq', 'ep')
The draws below stay inside these ranges and needn't reach their ends.
Inputs may be any that keep to these rules, and one draw needn't show every extreme that they name: `routes`: in each aligned block of 256 tokens (the tokens of one index of seq) no expert is named by more than 72 tokens, and in every draw some expert is named by exactly 72 tokens of some block; a token's two experts differ.
All inputs are finite; a program needn't handle non-finite values.
Results may differ from the reference program's by a relative error of at most 0.035.
Values may be sent and summed in bfloat16 or wider, within the bound.
No kernel may reach another device: no remote copies, remote signals or barrier semaphores. Data moves between devices by JAX's collectives and lax.ppermute only.
A program may use at most 128 MiB of HBM per device.

```python
import math
import jax
import jax.numpy as jnp
import numpy as np
from jax import lax

D = 6144
FF = 9216
HEAD_DIM = 128
TOK_DEV = 256
BLOCK = 256
HEADS = 32
EXPERTS = 8
TOKENS = 4096
CAP = 72
FF_DEV = 576
N_SEQ = 16


def log_uniform(key, shape, lowest, highest):
    return jnp.exp(jax.random.uniform(key, shape, jnp.float32, math.log(lowest), math.log(highest)))


def draw_log_decay(key, part):
    key = jax.random.fold_in(key, 11)
    subkeys = jax.random.split(key, 7)
    fast_share = 0.5
    is_fast = jax.random.uniform(subkeys[0], (HEADS, 1)) < fast_share
    fast_rate = log_uniform(subkeys[1], (HEADS, 1), 1.0 / 50.0, 1.0 / 30.0)
    slow_rate = log_uniform(subkeys[2], (HEADS, 1), 0.1, 0.4) / TOKENS
    fading_increment_ratio = jnp.where(is_fast, fast_rate, slow_rate)
    sections = TOKENS // TOK_DEV
    dispersion_extent = log_uniform(subkeys[3], (HEADS, sections, 1), 0.5, 2.0)
    dispersion_extent = jnp.broadcast_to(dispersion_extent, (HEADS, sections, TOK_DEV)).reshape(HEADS, TOKENS)
    gaussian_jitter = jax.random.uniform(subkeys[4], (HEADS, TOKENS), jnp.float32, 0.5, 1.5)
    places = jax.random.randint(subkeys[5], (HEADS, 1, 2), 0, TOKENS)
    objective_readings = jax.random.uniform(subkeys[6], (HEADS, 1, 2), jnp.float32, 0.22, 0.69)
    agreeing_locations = jnp.arange(TOKENS)[None, :, None] == places
    clustered_bunches = jnp.sum(jnp.where(agreeing_locations, objective_readings, 0.0), axis=2)
    return -(fading_increment_ratio * dispersion_extent * gaussian_jitter) - clustered_bunches


def draw_residual(key, part):
    key = jax.random.fold_in(key, 23)
    subkeys = jax.random.split(key, 3)
    rise_factor = 3.0
    normal_part = jax.random.truncated_normal(subkeys[0], -4.0, 4.0, (TOKENS, D), jnp.float32)
    row_scale = log_uniform(subkeys[1], (TOKENS, 1), 0.3, 3.0)
    column_place = jnp.arange(D, dtype=jnp.float32)[None, :] / (D - 1)
    column_scale = jnp.exp(column_place * math.log(rise_factor)) * log_uniform(subkeys[2], (1, D), 0.3, 1.0)
    return (normal_part * row_scale * column_scale).astype(jnp.bfloat16)


def levels(own_key, extent, cuts, low, largest):
    def one(axis_at, blocks):
        steps = jax.random.uniform(jax.random.fold_in(jax.random.fold_in(own_key, 6), axis_at), (blocks,), jnp.float32, low / len(cuts), largest / len(cuts))
        return jnp.repeat(jnp.exp(steps), extent[axis_at] // blocks).reshape((-1,) + (1,) * (len(extent) - axis_at - 1))

    loudness = one(*cuts[0])
    for cut in cuts[1:]:
        loudness = loudness * one(*cut)
    return loudness


def assign_block(rng, own, number, rows, number_of, top, reach, lean):
    order = jax.random.permutation(rng, number_of)
    crowded, common = portions_of(number_of, rows * top, reach, lean, True), portions_of(number_of, rows * top, reach, lean, False)
    places = jnp.arange(number_of)

    def named(sizes, offset_by):
        used = int((sizes > 0).sum())
        fixed = max(1, used // 4)
        moved = fixed + (places - fixed + offset_by * (used - fixed)) % max(1, number_of - fixed)
        return jnp.zeros((number_of,), jnp.int32).at[order[jnp.where(places < fixed, places, moved)]].set(jnp.asarray(sizes, jnp.int32))

    sizes = jnp.where(number % 4 == 0, named(crowded, number // 4), named(common, number - number // 4 - 1))
    mixed = jax.random.permutation(jax.random.fold_in(own, 3), number_of)
    donor, sink = mixed[0:number_of // 2 * 2:2], mixed[1:number_of // 2 * 2:2]
    slack = jnp.minimum(sizes[donor] - 1, reach - sizes[sink]) // 2
    slack = jnp.where((donor == order[0]) | (sink == order[0]) | (sizes[sink] == 0), 0, jnp.maximum(slack, 0))
    moved = jax.random.randint(jax.random.fold_in(own, 4), (number_of // 2,), 0, 1 << 20) % (slack + 1)
    sizes = sizes.at[donor].add(-moved).at[sink].add(moved)
    members = jnp.searchsorted(jnp.cumsum(sizes), jnp.arange(rows * top), side="right").astype(jnp.int32)
    listing = members.reshape(top, rows).T
    listing = listing[jax.random.permutation(jax.random.fold_in(own, 1), rows)]
    offset_by = jax.random.randint(jax.random.fold_in(own, 2), (rows, 1), 0, top)
    return jnp.take_along_axis(listing, (jnp.arange(top)[None, :] + offset_by) % top, axis=1)


def portions_of(count, total, reach, lean, full):
    loads = [(1 << 20) // math.isqrt(rank ** lean) + 1 for rank in range(1, count + 1)]
    largest = reach if full else min(reach, max(-(-total // count), total * loads[0] // sum(loads)))
    least = 1 if total - largest >= count - 1 else 0
    holding, spare = [largest] + [least] * (count - 1), total - largest - least * (count - 1)
    while spare > 0:
        candidates = [i for i in range(1, count) if holding[i] < largest] or [i for i in range(1, count) if holding[i] < reach]
        pool, left = sum([loads[i] for i in candidates]), spare
        for i in candidates:
            addition = min(reach - holding[i], max(1, left * loads[i] // pool), spare)
            holding[i] = holding[i] + addition
            spare = spare - addition
    return np.array(holding)


def scatter_about(own_key, shape, deviation, reach, cuts=(), held_as=jnp.bfloat16):
    factor_of = levels(own_key, shape, cuts, -0.22, 0.18) if cuts else 1.0
    array = jax.random.normal(own_key, shape, jnp.float32) * deviation * factor_of
    return jnp.minimum(jnp.maximum(array, -reach), reach).astype(held_as)


def setup_inputs(seed: int = 0) -> dict:
    splits = jax.random.split(jax.random.key(seed), 12)
    queries = scatter_about(splits[0], (TOKENS, HEADS * HEAD_DIM), 1.0, 6.0, ((0, 16), (1, 8)))
    key_rows = scatter_about(splits[1], (TOKENS, HEADS * HEAD_DIM), 1.0, 6.0, ((0, 16), (1, 8)))
    values = scatter_about(splits[2], (TOKENS, HEADS * HEAD_DIM), 1.0, 6.0, ((0, 16), (1, 8)))
    log_decay = draw_log_decay(jax.random.fold_in(splits[11], 71), 0)
    residual = draw_residual(jax.random.fold_in(splits[11], 71), 0)
    w_out = scatter_about(splits[5], (HEADS * HEAD_DIM, D), (HEADS * HEAD_DIM) ** -0.5, 0.09375, ((0, 8), (1, 16)))
    w_gate = scatter_about(splits[6], (EXPERTS, D, FF), D ** -0.5, 0.078125, ((0, 8), (2, 16)))
    w_up = scatter_about(splits[7], (EXPERTS, D, FF), D ** -0.5, 0.078125, ((0, 8), (2, 16)))
    w_down = scatter_about(splits[8], (EXPERTS, FF, D), FF ** -0.5, 0.0625, ((0, 8), (1, 16)))
    routes_keys = jax.random.split(jax.random.fold_in(splits[9], 1), TOKENS // TOK_DEV)
    routes_turns = jax.random.permutation(jax.random.fold_in(splits[9], 3), TOKENS // TOK_DEV)
    routes = jax.vmap(lambda own, number: assign_block(jax.random.fold_in(splits[9], 2), own, number, TOK_DEV, EXPERTS, 2, CAP, 2))(routes_keys, routes_turns).reshape((TOKENS, 2))
    gate_values = jnp.clip(0.1 + 0.9 * jax.random.uniform(splits[10], (TOKENS, 2), jnp.float32) ** levels(splits[10], (TOKENS, 2), ((0, 16),), -0.2, 0.2), 0.1, 1.0)
    return dict(queries=queries, key_rows=key_rows, values=values, log_decay=log_decay, residual=residual, w_out=w_out, w_gate=w_gate, w_up=w_up, w_down=w_down, routes=routes, gate_values=gate_values)


EPSILON = 1e-06

def block_parts(query_blocks, key_blocks, value_blocks, decays):
    inv_dim = 1.0 / query_blocks.shape[-1]
    width = decays.shape[2]
    cumulative = jnp.cumsum(decays, axis=2)
    block_total = cumulative[:, :, -1]
    later_pos = lax.broadcasted_iota(jnp.int32, (width, width), 0)
    earlier_pos = lax.broadcasted_iota(jnp.int32, (width, width), 1)
    causal = later_pos >= earlier_pos
    dispersion_extent = cumulative[:, :, :, None] - cumulative[:, :, None, :]
    decay_grid = jnp.where(causal, jnp.exp(jnp.where(causal, dispersion_extent, 0.0)), 0.0)
    scores = jnp.einsum('bthd,bshd->bhts', query_blocks.astype(jnp.float32), key_blocks.astype(jnp.float32))
    weights = (scores * (decay_grid * inv_dim)).astype(jnp.bfloat16)
    within = jnp.einsum('bhts,bshd->bthd', weights.astype(jnp.float32), value_blocks.astype(jnp.float32))
    carry_decay = jnp.transpose(jnp.exp(block_total[:, :, None] - cumulative), (0, 2, 1))
    keyed = (key_blocks.astype(jnp.float32) * carry_decay[..., None]).astype(jnp.bfloat16)
    update = jnp.einsum('bshd,bshe->bhde', keyed.astype(jnp.float32), value_blocks.astype(jnp.float32))
    return (cumulative, block_total, within, update)

def reference(queries, key_rows, values, log_decay, residual, w_out, w_gate, w_up, w_down, routes, gate_values):
    blocks = TOKENS // BLOCK
    block_shape = (blocks, BLOCK, HEADS, HEAD_DIM)
    query_blocks = queries.reshape(block_shape)
    decays = jnp.transpose(log_decay.reshape(HEADS, blocks, BLOCK), (1, 0, 2))
    cumulative, block_total, within, update = block_parts(query_blocks, key_rows.reshape(block_shape), values.reshape(block_shape), decays)

    def advance(state, pieces):
        return (jnp.exp(pieces[0])[:, None, None] * state + pieces[1], state)
    _, states = lax.scan(advance, jnp.zeros((HEADS, HEAD_DIM, HEAD_DIM), jnp.float32), (block_total, update))
    readout = jnp.einsum('bthd,bhde->bthe', query_blocks.astype(jnp.float32), states, precision=lax.Precision.HIGHEST)
    carried = jnp.transpose(jnp.exp(cumulative), (0, 2, 1))[..., None] * readout * (1.0 / HEAD_DIM)
    attention = (within + carried).astype(jnp.bfloat16).reshape(TOKENS, HEADS * HEAD_DIM)
    projected = jnp.dot(attention, w_out, preferred_element_type=jnp.float32)
    stream = (residual.astype(jnp.float32) + projected).astype(jnp.bfloat16)
    widened = stream.astype(jnp.float32)
    norm_scale = lax.rsqrt(lax.optimization_barrier(jnp.mean(widened * widened, axis=1)) + EPSILON)
    normed = (widened * norm_scale[:, None]).astype(jnp.bfloat16)
    normed_rows = normed.reshape(N_SEQ, TOK_DEV, D).astype(jnp.float32)
    route_rows = routes.reshape(N_SEQ, TOK_DEV, 2)
    weight_rows = gate_values.reshape(N_SEQ, TOK_DEV, 2)
    slot_ids = jnp.arange(CAP, dtype=jnp.int32)

    def one_expert(accumulated, expert):
        is_named = jnp.any(route_rows == expert, axis=2)
        slot_rank = jnp.cumsum(is_named.astype(jnp.int32), axis=1) - 1
        chosen = (is_named[:, None, :] & (slot_rank[:, None, :] == slot_ids[None, :, None])).astype(jnp.float32)
        packed = jnp.einsum('sct,std->scd', chosen, normed_rows, precision=lax.Precision.HIGHEST)
        packed = packed.astype(jnp.bfloat16).reshape(N_SEQ * CAP, D)
        gate_pre = jnp.dot(packed, w_gate[expert], preferred_element_type=jnp.float32)
        lifted = jnp.dot(packed, w_up[expert], preferred_element_type=jnp.float32)
        hidden = (jax.nn.silu(gate_pre) * lifted).astype(jnp.bfloat16)
        down_matrix = w_down[expert]

        def add_block(running, block_index):
            start_unit = (block_index * FF_DEV).astype(jnp.int32)
            row_block = lax.dynamic_slice_in_dim(hidden, start_unit, FF_DEV, 1)
            down_rows = lax.dynamic_slice_in_dim(down_matrix, start_unit, FF_DEV, 0)
            partial_value = lax.optimization_barrier(jnp.dot(row_block, down_rows, preferred_element_type=jnp.float32).astype(jnp.bfloat16))
            return (running + partial_value.astype(jnp.float32), None)
        outputs, _ = lax.scan(add_block, jnp.zeros((N_SEQ * CAP, D), jnp.float32), jnp.arange(N_SEQ, dtype=jnp.int32))
        outputs = outputs.reshape(N_SEQ, CAP, D)
        weight = lax.optimization_barrier(jnp.sum(jnp.where(route_rows == expert, weight_rows, 0.0), axis=2))
        slot_index = jnp.clip(slot_rank, 0, CAP - 1).astype(jnp.int32)
        picked = jnp.take_along_axis(outputs, slot_index[:, :, None], axis=1)
        return (accumulated + weight[:, :, None] * picked, None)
    mixture, _ = lax.scan(one_expert, jnp.zeros((N_SEQ, TOK_DEV, D), jnp.float32), jnp.arange(EXPERTS, dtype=jnp.int32))
    expert_mix = mixture.reshape(TOKENS, D).astype(jnp.bfloat16)
    return (attention, expert_mix)
```

```python
import functools

import jax
import jax.numpy as jnp
from jax import lax
from jax.experimental import pallas as pl
from jax.experimental.pallas import tpu as pltpu
from jax.sharding import PartitionSpec as P

HEAD_DIM = 128
EPSILON = 1e-06
SIDE = 4
CORES = 2
BF = jnp.bfloat16
F32 = jnp.float32


def pairs(move):
    out = []
    for z in range(SIDE):
        for y in range(SIDE):
            for x in range(SIDE):
                for c in range(CORES):
                    source = ((z * SIDE + y) * SIDE + x) * CORES + c
                    place = move(z, y, x, c)
                    if place is None:
                        continue
                    tz, ty, tx, tc = place
                    tz, ty, tx, tc = tz % SIDE, ty % SIDE, tx % SIDE, tc % CORES
                    out.append((source, ((tz * SIDE + ty) * SIDE + tx) * CORES + tc))
    return out


def send(value, move):
    return lax.ppermute(value, ("seq", "ep"), pairs(move))


def shift(value, axis, d):
    def move(z, y, x, c):
        if (axis == "a") == (c == 0):
            return z, y + d, x, c
        return z + d, y, x, c

    return send(value, move)


def gather_pair(block, axis):
    far = shift(block, axis, 2)
    return block, shift(block, axis, -1), far, shift(block, axis, 1)


def gather_halves(top, bottom, axis, after=None):
    top_1, bottom_3 = shift(top, axis, -1), shift(bottom, axis, 1)
    if after is not None:
        top, bottom, _ = lax.optimization_barrier((top, bottom, after))
    bottom_1, top_3 = shift(bottom, axis, -1), shift(top, axis, 1)
    top_2 = shift(top_1, axis, -1)
    bottom_2 = shift(bottom_3, axis, 1)
    return (top, bottom), (top_1, bottom_1), (top_2, bottom_2), (top_3, bottom_3)


def add(*parts):
    return functools.reduce(lambda a, b: a + b, [p.astype(F32) for p in parts])


def line_state(log_total, state, move_of):
    rows = state.reshape(-1, HEAD_DIM).astype(BF)
    high = log_total.astype(BF)
    mid = (log_total - high.astype(F32)).astype(BF)
    low = (log_total - high.astype(F32) - mid.astype(F32)).astype(BF)
    heads = log_total.shape[0]
    extra = jnp.zeros((16, HEAD_DIM), BF)
    extra = extra.at[0, :heads].set(high).at[1, :heads].set(mid).at[2, :heads].set(low)
    message = jnp.concatenate([rows, extra], axis=0)
    got = [send(message, move_of(d)) for d in range(1, SIDE)]

    def parse(m):
        t = m[-16:-13, :heads].astype(F32).sum(axis=0)
        return t, m[:-16].astype(F32).reshape(state.shape)

    return [(log_total, state)] + [parse(m) for m in got], got


def chain(earlier, later):
    return (
        earlier[0] + later[0],
        jnp.exp(later[0])[:, None, None] * earlier[1] + later[1],
    )


def entering_state(log_total, state, z, y):
    line, _ = line_state(
        log_total, state, lambda d: lambda pz, py, px, pc: (pz, py + d, px, pc)
    )

    def masked(part, keep):
        return jnp.where(keep, part[0], 0.0), jnp.where(keep, part[1], 0.0)

    def prefix(parts, place):
        total = (jnp.zeros_like(log_total), jnp.zeros_like(state))
        for d in range(SIDE - 1, 0, -1):
            total = chain(total, masked(parts[d], d <= place))
        return total

    before_y = prefix(line, y)
    after = (jnp.zeros_like(log_total), jnp.zeros_like(state))
    for d in range(SIDE - 1, 0, -1):
        after = chain(after, masked(line[d], d > y))
    whole = chain(chain(before_y, line[0]), after)
    lines, messages = line_state(
        whole[0], whole[1], lambda d: lambda pz, py, px, pc: (pz + d, py, px, pc)
    )
    before_z = prefix(lines, z)
    return chain(before_z, before_y)[1], messages


def project_kernel(groups, has_buffer, table, rows, *rest):
    columns = rest[:groups]
    mine, other, product, sems = rest[-4:]
    half, width = product.shape[0] // groups, product.shape[2]
    experts = mine.shape[0]

    def copy_out(i, dest, t):
        place = dest.at[t // 2, :, pl.ds(pl.multiple_of((t % 2) * width, 128), width)]
        return pltpu.make_async_copy(product.at[i], place, sems.at[i])

    for i in range(groups * half):
        product[i] = jnp.dot(
            rows[...], columns[i // half][i % half], preferred_element_type=F32
        ).astype(BF)
        t = table[i]

        @pl.when(t < 2 * experts)
        def _():
            copy_out(i, mine, t).start()

        @pl.when(t >= 2 * experts)
        def _():
            copy_out(i, other, t - 2 * experts).start()

    for i in range(groups * half):
        copy_out(i, mine, 0).wait()


def project(rows, columns, table, buffers):
    groups = len(columns)
    half, depth, width = columns[0].shape
    tokens = rows.shape[0]
    count = groups * half
    any_spec = pl.BlockSpec(memory_space=pl.ANY)
    vmem = pl.BlockSpec(memory_space=pltpu.VMEM)
    operands = [table, rows, *columns]
    in_specs = [pl.BlockSpec(memory_space=pltpu.SMEM), vmem] + [vmem] * groups
    aliases = {}
    if buffers is not None:
        operands += list(buffers)
        in_specs += [any_spec, any_spec]
        aliases = {2 + groups: 0, 3 + groups: 1}
    result = jax.ShapeDtypeStruct((SIDE, tokens, 2 * width), BF)
    return pl.pallas_call(
        functools.partial(project_kernel, groups, buffers is not None),
        out_shape=(result, result),
        in_specs=in_specs,
        out_specs=(any_spec, any_spec),
        scratch_shapes=[
            pltpu.VMEM((count, tokens, width), BF),
            pltpu.SemaphoreType.DMA((count,)),
        ],
        input_output_aliases=aliases,
        compiler_params=pltpu.CompilerParams(vmem_limit_bytes=24 * 1024 * 1024),
        cost_estimate=pl.CostEstimate(
            flops=2 * count * tokens * depth * width,
            bytes_accessed=2 * count * (depth * width + tokens * width),
            transcendentals=0,
        ),
        name="project",
    )(*operands)


def expert_kernel(count, steps, *refs):
    xs, (w_gate, w_up, w_down) = refs[:count], refs[count : count + 3]
    outs = refs[count + 3 : 2 * count + 3]
    gate, up, hidden = refs[2 * count + 3 :]
    rows = xs[0].shape[0]
    i = pl.program_id(0)

    def product(w):
        x = jnp.concatenate([r[...] for r in xs], axis=0)
        return lax.dot_general(x, w[...], (((1,), (1,)), ((), ())), preferred_element_type=F32)

    @pl.when(i == 0)
    def _():
        gate[...] = product(w_gate)
        up[...] = product(w_up)

    @pl.when((i > 0) & (i < steps))
    def _():
        gate[...] += product(w_gate)
        up[...] += product(w_up)

    @pl.when(i == steps - 1)
    def _():
        g = gate[...]
        hidden[...] = (g / (1.0 + jnp.exp(-g)) * up[...]).astype(BF)

    @pl.when(i >= steps)
    def _():
        out = jnp.dot(hidden[...], w_down[...], preferred_element_type=F32).astype(BF)
        for n in range(count):
            outs[n][...] = out[n * rows : (n + 1) * rows]


def expert(blocks, w_gate, w_up, w_down):
    count = len(blocks)
    rows, model = blocks[0].shape
    units = w_gate.shape[0]
    tile = 2048
    steps = model // tile
    early = lambda i: jnp.minimum(i, steps - 1)
    late = lambda i: jnp.maximum(i - steps, 0)
    result = jax.ShapeDtypeStruct((rows, model), BF)
    return pl.pallas_call(
        functools.partial(expert_kernel, count, steps),
        out_shape=[result] * count,
        grid=(2 * steps,),
        in_specs=[pl.BlockSpec((rows, tile), lambda i: (0, early(i)))] * count
        + [pl.BlockSpec((units, tile), lambda i: (0, early(i)))] * 2
        + [pl.BlockSpec((units, tile), lambda i: (0, late(i)))],
        out_specs=[pl.BlockSpec((rows, tile), lambda i: (0, late(i)))] * count,
        scratch_shapes=[
            pltpu.VMEM((count * rows, units), F32),
            pltpu.VMEM((count * rows, units), F32),
            pltpu.VMEM((count * rows, units), BF),
        ],
        compiler_params=pltpu.CompilerParams(vmem_limit_bytes=40 * 1024 * 1024),
        cost_estimate=pl.CostEstimate(
            flops=6 * count * rows * model * units,
            bytes_accessed=2 * (3 * model * units + 2 * count * rows * model),
            transcendentals=count * rows * units,
        ),
        name="expert",
    )(*blocks, w_gate, w_up, w_down)


def local_attention(queries, key_rows, values, log_decay):
    heads = log_decay.shape[0]
    length = queries.shape[0]
    shape = (length, heads, HEAD_DIM)
    q, k, v = (a.reshape(shape) for a in (queries, key_rows, values))
    later = lax.broadcasted_iota(jnp.int32, (length, length), 0)
    earlier = lax.broadcasted_iota(jnp.int32, (length, length), 1)
    causal = later >= earlier
    cumulative = jnp.cumsum(log_decay, axis=1)
    log_total = cumulative[:, -1]
    fall = jnp.exp(log_total[:, None] - cumulative).T
    keyed = (k.astype(F32) * fall[..., None]).astype(BF)
    update = jnp.einsum("shd,she->hde", keyed, v, preferred_element_type=F32)
    spread = cumulative[:, :, None] - cumulative[:, None, :]
    grid = jnp.where(causal, jnp.exp(jnp.where(causal, spread, 0.0)), 0.0)
    scores = jnp.einsum("thd,shd->hts", q, k, preferred_element_type=F32)
    weights = (scores * (grid * (1.0 / HEAD_DIM))).astype(BF)
    within = jnp.einsum("hts,shd->thd", weights, v, preferred_element_type=F32)
    return cumulative, log_total, update, within, q


def shards(
    queries, key_rows, values, log_decay, residual, w_out, w_gate, w_up, w_down, routes, gate_values
):
    length = queries.shape[0]
    heads = log_decay.shape[0]
    place, own = lax.axis_index("seq"), lax.axis_index("ep")
    z, y = place // SIDE, place % SIDE
    x, c = own // CORES, own % CORES
    pos_a = jnp.where(c == 0, y, z)
    pos_b = jnp.where(c == 0, z, y)

    w0, w1, w2, w3 = gather_pair(w_out, "a")
    w_top, w_bottom = jnp.stack([w0, w1]), jnp.stack([w2, w3])

    cumulative, log_total, update, within, q = local_attention(
        queries, key_rows, values, log_decay
    )
    state, messages = entering_state(log_total, update, z, y)
    g0, g1, g2, g3 = gather_halves(w_top, w_bottom, "b", messages)
    readout = jnp.einsum(
        "thd,hde->the", q.astype(F32), state, precision=lax.Precision.HIGHEST
    )
    carried = jnp.exp(cumulative).T[..., None] * readout * (1.0 / HEAD_DIM)
    attention = (within + carried).astype(BF).reshape(length, heads * HEAD_DIM)

    def table(offsets):
        a = (pos_a + jnp.array([o[0] for o in offsets])) % SIDE
        b = (pos_b + jnp.array([o[1] for o in offsets])) % SIDE
        j = jnp.where(c == 0, b * SIDE + a, a * SIDE + b)
        e = j // 2
        return ((((e % 2) != c) * SIDE + (e // 2 - x) % SIDE) * 2 + j % 2).astype(jnp.int32)

    everyone = lambda *bs: table([(a, b) for b in bs for a in range(SIDE)])
    partial = project(attention, g0, everyone(0), None)
    partial = project(attention, g1 + g3, everyone(1, 3), partial)
    partial = project(attention, g2, everyone(2), partial)

    other = send(partial[1], lambda pz, py, px, pc: (pz, py, px, pc + 1))
    both = [add(partial[0][d], other[d]) for d in range(SIDE)]
    arrived = [
        send(both[d].astype(BF), functools.partial(lambda d, pz, py, px, pc: (pz, py, px + d, pc), d))
        for d in range(1, SIDE)
    ]
    stream = add(residual, both[0], *arrived).astype(BF)

    experts = lax.axis_size("ep")
    capacity = length * 9 // (4 * experts)
    ids = jnp.arange(experts, dtype=jnp.int32)
    named = routes[None, :, :] == ids[:, None, None]
    is_named = jnp.any(named, axis=2)
    rank = jnp.cumsum(is_named.astype(jnp.int32), axis=1) - 1
    slots = jnp.arange(capacity, dtype=jnp.int32)
    chosen = is_named[:, None, :] & (rank[:, None, :] == slots[None, :, None])
    weight = jnp.sum(jnp.where(named, gate_values[None], 0.0), axis=2)

    width = stream.shape[1]
    wide = stream.astype(F32)
    squares = jnp.sum(wide * wide, axis=1, keepdims=True)
    s0 = squares.astype(BF).astype(F32)
    s1 = (squares - s0).astype(BF).astype(F32)
    s2 = squares - s0 - s1
    lane = lax.broadcasted_iota(jnp.int32, (length, 128), 1)
    tail = jnp.where(lane == 0, s0, jnp.where(lane == 1, s1, jnp.where(lane == 2, s2, 0.0)))
    rows = jnp.concatenate([stream, tail.astype(BF)], axis=1)
    picked = jnp.dot(
        chosen.astype(BF).reshape(experts * capacity, length), rows, preferred_element_type=F32
    ).astype(BF)
    got = lax.all_to_all(picked.reshape(experts, capacity, width + 128), "ep", 0, 0)
    square_sum = jnp.sum(got[:, :, width : width + 3].astype(F32), axis=(0, 2))
    scale = lax.rsqrt(square_sum / (experts * width) + EPSILON)
    normed = (got[:, :, :width].astype(F32) * scale[None, :, None]).astype(BF)
    packed = jnp.transpose(normed, (1, 0, 2)).reshape(capacity, experts * width)

    c0, c1, c2, c3 = gather_pair(packed, "a")
    r0, r1, r2, r3 = gather_halves(
        jnp.concatenate([c0, c1], axis=0), jnp.concatenate([c2, c3], axis=0), "b"
    )
    weights = (w_gate[0].T, w_up[0].T, w_down[0])
    top_0, bottom_0 = expert(r0, *weights)
    top_1, bottom_1, top_3, bottom_3 = expert(r1 + r3, *weights)
    top_2, bottom_2 = expert(r2, *weights)
    far_3, far_1 = shift(top_3, "b", -1), shift(bottom_1, "b", 1)
    sum_1 = add(top_1, shift(top_2, "b", 1)).astype(BF)
    sum_3 = add(bottom_3, shift(bottom_2, "b", -1)).astype(BF)
    top = add(top_0, far_3, shift(sum_1, "b", 1))
    bottom = add(bottom_0, far_1, shift(sum_3, "b", -1))
    mine = add(
        top[:capacity],
        shift(top[capacity:].astype(BF), "a", 1),
        shift(bottom[:capacity].astype(BF), "a", 2),
        shift(bottom[capacity:].astype(BF), "a", -1),
    ).astype(BF)

    returned = lax.all_to_all(
        jnp.transpose(mine.reshape(capacity, experts, width), (1, 0, 2)), "ep", 0, 0
    )
    w_hi = weight.astype(BF).astype(F32)
    w_lo = weight - w_hi
    spread = jnp.concatenate(
        [jnp.where(chosen, w[:, None, :], 0.0).astype(BF) for w in (w_hi, w_lo)], axis=0
    ).reshape(2 * experts * capacity, length)
    flat = returned.reshape(experts * capacity, width)
    mix = lax.dot_general(
        spread,
        jnp.concatenate([flat, flat], axis=0),
        (((0,), (0,)), ((), ())),
        preferred_element_type=F32,
    )
    return attention, mix.astype(BF)


def solution(mesh):
    placed = (
        P("seq", "ep"),
        P("seq", "ep"),
        P("seq", "ep"),
        P("ep", "seq"),
        P("seq", "ep"),
        P("ep", "seq"),
        P("ep", None, "seq"),
        P("ep", None, "seq"),
        P("ep", "seq", None),
        P("seq", None),
        P("seq", None),
    )
    return jax.shard_map(
        shards,
        mesh=mesh,
        in_specs=placed,
        out_specs=(P("seq", "ep"), P("seq", "ep")),
        check_vma=False,
    )
```

```python
import functools

import jax
import jax.numpy as jnp
from jax import lax
from jax.experimental import pallas as pl
from jax.experimental.pallas import tpu as pltpu
from jax.sharding import PartitionSpec as P

HEAD_DIM = 128
EPSILON = 1e-06
SIDE = 4
CORES = 2
BF = jnp.bfloat16
F32 = jnp.float32


def pairs(move):
    out = []
    for z in range(SIDE):
        for y in range(SIDE):
            for x in range(SIDE):
                for c in range(CORES):
                    source = ((z * SIDE + y) * SIDE + x) * CORES + c
                    place = move(z, y, x, c)
                    if place is None:
                        continue
                    tz, ty, tx, tc = place
                    tz, ty, tx, tc = tz % SIDE, ty % SIDE, tx % SIDE, tc % CORES
                    out.append((source, ((tz * SIDE + ty) * SIDE + tx) * CORES + tc))
    return out


def send(value, move):
    return lax.ppermute(value, ("seq", "ep"), pairs(move))


def shift(value, axis, d, name="block"):
    def move(z, y, x, c):
        if (axis == "a") == (c == 0):
            return z, y + d, x, c
        return z + d, y, x, c

    with jax.named_scope(name):
        return send(value, move)


def gather_pair(block, axis):
    far = shift(block, axis, 2, "pair_2")
    return block, shift(block, axis, -1, "pair_1"), far, shift(block, axis, 1, "pair_3")


def gather_halves(top, bottom, axis, after=None):
    top_1, bottom_3 = shift(top, axis, -1, "top_1"), shift(bottom, axis, 1, "bottom_3")
    if after is not None:
        top, bottom, _ = lax.optimization_barrier((top, bottom, after))
    bottom_1, top_3 = shift(bottom, axis, -1, "bottom_1"), shift(top, axis, 1, "top_3")
    top_2 = shift(top_1, axis, -1, "top_2")
    bottom_2 = shift(bottom_3, axis, 1, "bottom_2")
    return (top, bottom), (top_1, bottom_1), (top_2, bottom_2), (top_3, bottom_3)


def ring_rows(left, right, name, beside=None):
    left_1, right_3 = shift(left, "b", -1, name + "_left_1"), shift(right, "b", 1, name + "_right_3")
    right_1, left_3 = shift(right, "b", -1, name + "_right_1"), shift(left, "b", 1, name + "_left_3")
    if beside is not None:
        left_1, right_1, left_3, right_3, beside = lax.optimization_barrier(
            (left_1, right_1, left_3, right_3, beside)
        )
    left_2 = shift(left_1, "b", -1, name + "_left_2")
    right_2 = shift(right_3, "b", 1, name + "_right_2")
    return [left, left_1, left_2, left_3], [right, right_1, right_2, right_3], beside


def ring_sums(lefts, rights, name, beside=None):
    from_2l, far_3 = shift(lefts[2], "b", 1, name + "_left_2"), shift(lefts[3], "b", -1, name + "_left_3")
    from_2r, far_1 = shift(rights[2], "b", -1, name + "_right_2"), shift(rights[1], "b", 1, name + "_right_1")
    if beside is not None:
        from_2l, from_2r, far_1, far_3, beside = lax.optimization_barrier(
            (from_2l, from_2r, far_1, far_3, beside)
        )
    near_1 = shift(add(lefts[1], from_2l).astype(BF), "b", 1, name + "_left_1")
    near_3 = shift(add(rights[3], from_2r).astype(BF), "b", -1, name + "_right_3")
    return add(lefts[0], far_3, near_1), add(rights[0], far_1, near_3), beside


def add(*parts):
    return functools.reduce(lambda a, b: a + b, [p.astype(F32) for p in parts])


def line_state(log_total, state, move_of):
    rows = state.reshape(-1, HEAD_DIM).astype(BF)
    high = log_total.astype(BF)
    mid = (log_total - high.astype(F32)).astype(BF)
    low = (log_total - high.astype(F32) - mid.astype(F32)).astype(BF)
    heads = log_total.shape[0]
    extra = jnp.zeros((16, HEAD_DIM), BF)
    extra = extra.at[0, :heads].set(high).at[1, :heads].set(mid).at[2, :heads].set(low)
    message = jnp.concatenate([rows, extra], axis=0)
    got = [send(message, move_of(d)) for d in range(1, SIDE)]

    def parse(m):
        t = m[-16:-13, :heads].astype(F32).sum(axis=0)
        return t, m[:-16].astype(F32).reshape(state.shape)

    return [(log_total, state)] + [parse(m) for m in got], got


def chain(earlier, later):
    return (
        earlier[0] + later[0],
        jnp.exp(later[0])[:, None, None] * earlier[1] + later[1],
    )


def entering_state(log_total, state, z, y, w_top, w_bottom):
    line, _ = line_state(
        log_total, state, lambda d: lambda pz, py, px, pc: (pz, py + d, px, pc)
    )

    def masked(part, keep):
        return jnp.where(keep, part[0], 0.0), jnp.where(keep, part[1], 0.0)

    def prefix(parts, place):
        total = (jnp.zeros_like(log_total), jnp.zeros_like(state))
        for d in range(SIDE - 1, 0, -1):
            total = chain(total, masked(parts[d], d <= place))
        return total

    before_y = prefix(line, y)
    after = (jnp.zeros_like(log_total), jnp.zeros_like(state))
    for d in range(SIDE - 1, 0, -1):
        after = chain(after, masked(line[d], d > y))
    whole = chain(chain(before_y, line[0]), after)
    whole, w_top, w_bottom = lax.optimization_barrier((whole, w_top, w_bottom))
    lines, messages = line_state(
        whole[0], whole[1], lambda d: lambda pz, py, px, pc: (pz + d, py, px, pc)
    )
    before_z = prefix(lines, z)
    return chain(before_z, before_y)[1], messages, w_top, w_bottom


def project_kernel(groups, has_buffer, table, rows, *rest):
    columns = rest[:groups]
    mine, other, product, sems = rest[-4:]
    half, width = product.shape[0] // groups, product.shape[2]
    experts = mine.shape[0]

    def copy_out(i, dest, t):
        place = dest.at[t // 2, :, pl.ds(pl.multiple_of((t % 2) * width, 128), width)]
        return pltpu.make_async_copy(product.at[i], place, sems.at[i])

    for i in range(groups * half):
        product[i] = jnp.dot(
            rows[...], columns[i // half][i % half], preferred_element_type=F32
        ).astype(BF)
        t = table[i]

        @pl.when(t < 2 * experts)
        def _():
            copy_out(i, mine, t).start()

        @pl.when(t >= 2 * experts)
        def _():
            copy_out(i, other, t - 2 * experts).start()

    for i in range(groups * half):
        copy_out(i, mine, 0).wait()


def project(rows, columns, table, buffers):
    groups = len(columns)
    half, depth, width = columns[0].shape
    tokens = rows.shape[0]
    count = groups * half
    any_spec = pl.BlockSpec(memory_space=pl.ANY)
    vmem = pl.BlockSpec(memory_space=pltpu.VMEM)
    operands = [table, rows, *columns]
    in_specs = [pl.BlockSpec(memory_space=pltpu.SMEM), vmem] + [vmem] * groups
    aliases = {}
    if buffers is not None:
        operands += list(buffers)
        in_specs += [any_spec, any_spec]
        aliases = {2 + groups: 0, 3 + groups: 1}
    result = jax.ShapeDtypeStruct((SIDE, tokens, 2 * width), BF)
    return pl.pallas_call(
        functools.partial(project_kernel, groups, buffers is not None),
        out_shape=(result, result),
        in_specs=in_specs,
        out_specs=(any_spec, any_spec),
        scratch_shapes=[
            pltpu.VMEM((count, tokens, width), BF),
            pltpu.SemaphoreType.DMA((count,)),
        ],
        input_output_aliases=aliases,
        compiler_params=pltpu.CompilerParams(vmem_limit_bytes=24 * 1024 * 1024),
        cost_estimate=pl.CostEstimate(
            flops=2 * count * tokens * depth * width,
            bytes_accessed=2 * count * (depth * width + tokens * width),
            transcendentals=0,
        ),
        name="project",
    )(*operands)


def lift_kernel(count, steps, *refs):
    lefts, rights = refs[:count], refs[count : 2 * count]
    w_gate, w_up, hidden, gate, up = refs[2 * count :]
    i = pl.program_id(0)

    def step(xs, first):
        x = jnp.concatenate([r[...] for r in xs], axis=0)
        for w, total in ((w_gate, gate), (w_up, up)):
            part = lax.dot_general(
                x, w[...], (((1,), (1,)), ((), ())), preferred_element_type=F32
            )
            total[...] = part if first else total[...] + part

    @pl.when(i == 0)
    def _():
        step(lefts, True)

    @pl.when((i > 0) & (i < steps))
    def _():
        step(lefts, False)

    @pl.when(i >= steps)
    def _():
        step(rights, False)

    @pl.when(i == 2 * steps - 1)
    def _():
        g = gate[...]
        hidden[...] = (g / (1.0 + jnp.exp(-g)) * up[...]).astype(BF)


def lift(lefts, rights, w_gate, w_up):
    count = len(lefts)
    rows, half = lefts[0].shape
    units = w_gate.shape[0]
    tile = 1536
    steps = half // tile
    return pl.pallas_call(
        functools.partial(lift_kernel, count, steps),
        out_shape=jax.ShapeDtypeStruct((count * rows, units), BF),
        grid=(2 * steps,),
        in_specs=[pl.BlockSpec((rows, tile), lambda i: (0, jnp.minimum(i, steps - 1)))] * count
        + [pl.BlockSpec((rows, tile), lambda i: (0, jnp.maximum(i - steps, 0)))] * count
        + [pl.BlockSpec((units, tile), lambda i: (0, i))] * 2,
        out_specs=pl.BlockSpec((count * rows, units), lambda i: (0, 0)),
        scratch_shapes=[pltpu.VMEM((count * rows, units), F32)] * 2,
        compiler_params=pltpu.CompilerParams(vmem_limit_bytes=52 * 1024 * 1024),
        cost_estimate=pl.CostEstimate(
            flops=8 * count * rows * half * units,
            bytes_accessed=2 * (4 * half * units + count * rows * (2 * half + units)),
            transcendentals=count * rows * units,
        ),
        name="lift",
    )(*lefts, *rights, w_gate, w_up)


def lower_kernel(count, hidden, w_down, *outs):
    out = jnp.dot(hidden[...], w_down[...], preferred_element_type=F32).astype(BF)
    rows = out.shape[0] // count
    for n in range(count):
        outs[n][...] = out[n * rows : (n + 1) * rows]


def lower(hidden, w_down, count, side):
    units, model = w_down.shape
    rows = hidden.shape[0] // count
    tile = 1536
    steps = model // 2 // tile
    return pl.pallas_call(
        functools.partial(lower_kernel, count),
        out_shape=[jax.ShapeDtypeStruct((rows, model // 2), BF)] * count,
        grid=(steps,),
        in_specs=[
            pl.BlockSpec(hidden.shape, lambda i: (0, 0)),
            pl.BlockSpec((units, tile), lambda i: (0, side * steps + i)),
        ],
        out_specs=[pl.BlockSpec((rows, tile), lambda i: (0, i))] * count,
        compiler_params=pltpu.CompilerParams(vmem_limit_bytes=52 * 1024 * 1024),
        cost_estimate=pl.CostEstimate(
            flops=count * rows * model * units,
            bytes_accessed=model * units + count * rows * (model + 2 * units),
            transcendentals=0,
        ),
        name="lower",
    )(hidden, w_down)


def local_attention(queries, key_rows, values, log_decay):
    heads = log_decay.shape[0]
    length = queries.shape[0]
    shape = (length, heads, HEAD_DIM)
    q, k, v = (a.reshape(shape) for a in (queries, key_rows, values))
    later = lax.broadcasted_iota(jnp.int32, (length, length), 0)
    earlier = lax.broadcasted_iota(jnp.int32, (length, length), 1)
    causal = later >= earlier
    cumulative = jnp.cumsum(log_decay, axis=1)
    log_total = cumulative[:, -1]
    fall = jnp.exp(log_total[:, None] - cumulative).T
    keyed = (k.astype(F32) * fall[..., None]).astype(BF)
    update = jnp.einsum("shd,she->hde", keyed, v, preferred_element_type=F32)
    spread = cumulative[:, :, None] - cumulative[:, None, :]
    grid = jnp.where(causal, jnp.exp(jnp.where(causal, spread, 0.0)), 0.0)
    scores = jnp.einsum("thd,shd->hts", q, k, preferred_element_type=F32)
    weights = (scores * (grid * (1.0 / HEAD_DIM))).astype(BF)
    within = jnp.einsum("hts,shd->thd", weights, v, preferred_element_type=F32)
    return cumulative, log_total, update, within, q


def shards(
    queries, key_rows, values, log_decay, residual, w_out, w_gate, w_up, w_down, routes, gate_values
):
    length = queries.shape[0]
    heads = log_decay.shape[0]
    place, own = lax.axis_index("seq"), lax.axis_index("ep")
    z, y = place // SIDE, place % SIDE
    x, c = own // CORES, own % CORES
    pos_a = jnp.where(c == 0, y, z)
    pos_b = jnp.where(c == 0, z, y)

    w0, w1, w2, w3 = gather_pair(w_out, "a")
    w_top, w_bottom = jnp.stack([w0, w1]), jnp.stack([w2, w3])

    cumulative, log_total, update, within, q = local_attention(
        queries, key_rows, values, log_decay
    )
    state, messages, w_top, w_bottom = entering_state(log_total, update, z, y, w_top, w_bottom)
    g0, g1, g2, g3 = gather_halves(w_top, w_bottom, "b", messages)
    readout = jnp.einsum(
        "thd,hde->the", q.astype(F32), state, precision=lax.Precision.HIGHEST
    )
    carried = jnp.exp(cumulative).T[..., None] * readout * (1.0 / HEAD_DIM)
    attention = (within + carried).astype(BF).reshape(length, heads * HEAD_DIM)

    def table(offsets):
        a = (pos_a + jnp.array([o[0] for o in offsets])) % SIDE
        b = (pos_b + jnp.array([o[1] for o in offsets])) % SIDE
        j = jnp.where(c == 0, b * SIDE + a, a * SIDE + b)
        e = j // 2
        return ((((e % 2) != c) * SIDE + (e // 2 - x) % SIDE) * 2 + j % 2).astype(jnp.int32)

    everyone = lambda *bs: table([(a, b) for b in bs for a in range(SIDE)])
    partial = project(attention, g0, everyone(0), None)
    partial = project(attention, g1 + g3, everyone(1, 3), partial)
    partial = project(attention, g2, everyone(2), partial)

    other = send(partial[1], lambda pz, py, px, pc: (pz, py, px, pc + 1))
    both = [add(partial[0][d], other[d]) for d in range(SIDE)]
    arrived = [
        send(both[d].astype(BF), functools.partial(lambda d, pz, py, px, pc: (pz, py, px + d, pc), d))
        for d in range(1, SIDE)
    ]
    stream = add(residual, both[0], *arrived).astype(BF)

    experts = lax.axis_size("ep")
    capacity = length * 9 // (4 * experts)
    ids = jnp.arange(experts, dtype=jnp.int32)
    named = routes[None, :, :] == ids[:, None, None]
    is_named = jnp.any(named, axis=2)
    rank = jnp.cumsum(is_named.astype(jnp.int32), axis=1) - 1
    slots = jnp.arange(capacity, dtype=jnp.int32)
    chosen = is_named[:, None, :] & (rank[:, None, :] == slots[None, :, None])
    weight = jnp.sum(jnp.where(named, gate_values[None], 0.0), axis=2)

    width = stream.shape[1]
    wide = stream.astype(F32)
    squares = jnp.sum(wide * wide, axis=1, keepdims=True)
    s0 = squares.astype(BF).astype(F32)
    s1 = (squares - s0).astype(BF).astype(F32)
    s2 = squares - s0 - s1
    lane = lax.broadcasted_iota(jnp.int32, (length, 128), 1)
    tail = jnp.where(lane == 0, s0, jnp.where(lane == 1, s1, jnp.where(lane == 2, s2, 0.0)))
    rows = jnp.concatenate([stream, tail.astype(BF)], axis=1)
    picked = jnp.dot(
        chosen.astype(BF).reshape(experts * capacity, length), rows, preferred_element_type=F32
    ).astype(BF)
    got = lax.all_to_all(picked.reshape(experts, capacity, width + 128), "ep", 0, 0)
    square_sum = jnp.sum(got[:, :, width : width + 3].astype(F32), axis=(0, 2))
    scale = lax.rsqrt(square_sum / (experts * width) + EPSILON)
    normed = (got[:, :, :width].astype(F32) * scale[None, :, None]).astype(BF)
    packed = jnp.transpose(normed, (1, 0, 2)).reshape(capacity, experts * width)

    half = packed.shape[1] // 2
    c1, c3 = shift(packed, "a", -1, "pair_1"), shift(packed, "a", 1, "pair_3")
    halves = lambda m, n: [
        jnp.concatenate([p[:, i * half : (i + 1) * half] for p in (m, n)], axis=0) for i in range(2)
    ]
    odd_l, odd_r, _ = ring_rows(*halves(c1, c3), "odd")
    c2l = shift(c1[:, :half], "a", -1, "pair_2_left")
    c2r = shift(c3[:, half:], "a", 1, "pair_2_right")
    even_own = [
        jnp.concatenate([packed[:, :half], c2l], axis=0),
        jnp.concatenate([packed[:, half:], c2r], axis=0),
    ]
    even_own, _ = lax.optimization_barrier((even_own, (odd_l[1], odd_r[3])))
    gate_rows, up_rows, down = w_gate[0].T, w_up[0].T, w_down[0]
    hidden_odd = lift(odd_l, odd_r, gate_rows, up_rows)
    even_l, even_r, hidden_odd = ring_rows(*even_own, "even", hidden_odd)
    hidden_even = lift(even_l, even_r, gate_rows, up_rows)
    part_l, part_r = (lower(hidden_odd, down, SIDE, side) for side in range(2))
    sum_odd_l, sum_odd_r, hidden_even = ring_sums(part_l, part_r, "back_odd", hidden_even)
    part_l, part_r = (lower(hidden_even, down, SIDE, side) for side in range(2))
    sum_even_l, sum_even_r, _ = ring_sums(part_l, part_r, "back_even")
    rows_of = lambda sums, i: jnp.concatenate(
        [m[i * capacity : (i + 1) * capacity] for m in sums], axis=1
    )
    odd, even = (sum_odd_l, sum_odd_r), (sum_even_l, sum_even_r)
    mine = add(
        rows_of(even, 0),
        shift(rows_of(even, 1).astype(BF), "a", 2, "back_pair_2"),
        shift(rows_of(odd, 0).astype(BF), "a", 1, "back_pair_1"),
        shift(rows_of(odd, 1).astype(BF), "a", -1, "back_pair_3"),
    ).astype(BF)

    returned = lax.all_to_all(
        jnp.transpose(mine.reshape(capacity, experts, width), (1, 0, 2)), "ep", 0, 0
    )
    w_hi = weight.astype(BF).astype(F32)
    w_lo = weight - w_hi
    spread = jnp.concatenate(
        [jnp.where(chosen, w[:, None, :], 0.0).astype(BF) for w in (w_hi, w_lo)], axis=0
    ).reshape(2 * experts * capacity, length)
    flat = returned.reshape(experts * capacity, width)
    mix = lax.dot_general(
        spread,
        jnp.concatenate([flat, flat], axis=0),
        (((0,), (0,)), ((), ())),
        preferred_element_type=F32,
    )
    return attention, mix.astype(BF)


def solution(mesh):
    placed = (
        P("seq", "ep"),
        P("seq", "ep"),
        P("seq", "ep"),
        P("ep", "seq"),
        P("seq", "ep"),
        P("ep", "seq"),
        P("ep", None, "seq"),
        P("ep", None, "seq"),
        P("ep", "seq", None),
        P("seq", None),
        P("seq", None),
    )
    return jax.shard_map(
        shards,
        mesh=mesh,
        in_specs=placed,
        out_specs=(P("seq", "ep"), P("seq", "ep")),
        check_vma=False,
    )
```

```python
import functools

import jax
import jax.numpy as jnp
from jax import lax
from jax.experimental import pallas as pl
from jax.experimental.pallas import tpu as pltpu
from jax.sharding import PartitionSpec as P

HEAD_DIM = 128
EPSILON = 1e-06
SIDE = 4
CORES = 2
BF = jnp.bfloat16
F32 = jnp.float32


def pairs(move):
    out = []
    for z in range(SIDE):
        for y in range(SIDE):
            for x in range(SIDE):
                for c in range(CORES):
                    source = ((z * SIDE + y) * SIDE + x) * CORES + c
                    place = move(z, y, x, c)
                    if place is None:
                        continue
                    tz, ty, tx, tc = place
                    tz, ty, tx, tc = tz % SIDE, ty % SIDE, tx % SIDE, tc % CORES
                    out.append((source, ((tz * SIDE + ty) * SIDE + tx) * CORES + tc))
    return out


def send(value, move):
    return lax.ppermute(value, ("seq", "ep"), pairs(move))


def shift(value, axis, d, name="block"):
    def move(z, y, x, c):
        if (axis == "a") == (c == 0):
            return z, y + d, x, c
        return z + d, y, x, c

    with jax.named_scope(name):
        return send(value, move)


def gather_pair(block, axis):
    far = shift(block, axis, 2, "pair_2")
    return block, shift(block, axis, -1, "pair_1"), far, shift(block, axis, 1, "pair_3")


def gather_halves(top, bottom, axis, after=None):
    top_1, bottom_3 = shift(top, axis, -1, "top_1"), shift(bottom, axis, 1, "bottom_3")
    if after is not None:
        top, bottom, _ = lax.optimization_barrier((top, bottom, after))
    bottom_1, top_3 = shift(bottom, axis, -1, "bottom_1"), shift(top, axis, 1, "top_3")
    top_2 = shift(top_1, axis, -1, "top_2")
    bottom_2 = shift(bottom_3, axis, 1, "bottom_2")
    return (top, bottom), (top_1, bottom_1), (top_2, bottom_2), (top_3, bottom_3)


def ring_rows(left, right, name, beside=None):
    left_1, right_3 = shift(left, "b", -1, name + "_left_1"), shift(right, "b", 1, name + "_right_3")
    right_1, left_3 = shift(right, "b", -1, name + "_right_1"), shift(left, "b", 1, name + "_left_3")
    if beside is not None:
        left_1, right_3, beside = lax.optimization_barrier((left_1, right_3, beside))
    left_2 = shift(left_1, "b", -1, name + "_left_2")
    right_2 = shift(right_3, "b", 1, name + "_right_2")
    return [left, left_1, left_2, left_3], [right, right_1, right_2, right_3], beside


def ring_sums(lefts, rights, name, beside=None):
    from_2l, far_3 = shift(lefts[2], "b", 1, name + "_left_2"), shift(lefts[3], "b", -1, name + "_left_3")
    from_2r, far_1 = shift(rights[2], "b", -1, name + "_right_2"), shift(rights[1], "b", 1, name + "_right_1")
    if beside is not None:
        from_2l, from_2r, beside = lax.optimization_barrier((from_2l, from_2r, beside))
    near_1 = shift(add(lefts[1], from_2l).astype(BF), "b", 1, name + "_left_1")
    near_3 = shift(add(rights[3], from_2r).astype(BF), "b", -1, name + "_right_3")
    return add(lefts[0], far_3, near_1), add(rights[0], far_1, near_3), beside


def add(*parts):
    return functools.reduce(lambda a, b: a + b, [p.astype(F32) for p in parts])


def line_state(log_total, state, move_of):
    rows = state.reshape(-1, HEAD_DIM).astype(BF)
    high = log_total.astype(BF)
    mid = (log_total - high.astype(F32)).astype(BF)
    low = (log_total - high.astype(F32) - mid.astype(F32)).astype(BF)
    heads = log_total.shape[0]
    extra = jnp.zeros((16, HEAD_DIM), BF)
    extra = extra.at[0, :heads].set(high).at[1, :heads].set(mid).at[2, :heads].set(low)
    message = jnp.concatenate([rows, extra], axis=0)
    got = [send(message, move_of(d)) for d in range(1, SIDE)]

    def parse(m):
        t = m[-16:-13, :heads].astype(F32).sum(axis=0)
        return t, m[:-16].astype(F32).reshape(state.shape)

    return [(log_total, state)] + [parse(m) for m in got], got


def chain(earlier, later):
    return (
        earlier[0] + later[0],
        jnp.exp(later[0])[:, None, None] * earlier[1] + later[1],
    )


def entering_state(log_total, state, z, y, w_top, w_bottom):
    line, _ = line_state(
        log_total, state, lambda d: lambda pz, py, px, pc: (pz, py + d, px, pc)
    )

    def masked(part, keep):
        return jnp.where(keep, part[0], 0.0), jnp.where(keep, part[1], 0.0)

    def prefix(parts, place):
        total = (jnp.zeros_like(log_total), jnp.zeros_like(state))
        for d in range(SIDE - 1, 0, -1):
            total = chain(total, masked(parts[d], d <= place))
        return total

    before_y = prefix(line, y)
    after = (jnp.zeros_like(log_total), jnp.zeros_like(state))
    for d in range(SIDE - 1, 0, -1):
        after = chain(after, masked(line[d], d > y))
    whole = chain(chain(before_y, line[0]), after)
    whole, w_top, w_bottom = lax.optimization_barrier((whole, w_top, w_bottom))
    lines, messages = line_state(
        whole[0], whole[1], lambda d: lambda pz, py, px, pc: (pz + d, py, px, pc)
    )
    before_z = prefix(lines, z)
    return chain(before_z, before_y)[1], messages, w_top, w_bottom


def project_kernel(groups, has_buffer, table, rows, *rest):
    columns = rest[:groups]
    mine, other, product, sems = rest[-4:]
    half, width = product.shape[0] // groups, product.shape[2]
    experts = mine.shape[0]

    def copy_out(i, dest, t):
        place = dest.at[t // 2, :, pl.ds(pl.multiple_of((t % 2) * width, 128), width)]
        return pltpu.make_async_copy(product.at[i], place, sems.at[i])

    for i in range(groups * half):
        product[i] = jnp.dot(
            rows[...], columns[i // half][i % half], preferred_element_type=F32
        ).astype(BF)
        t = table[i]

        @pl.when(t < 2 * experts)
        def _():
            copy_out(i, mine, t).start()

        @pl.when(t >= 2 * experts)
        def _():
            copy_out(i, other, t - 2 * experts).start()

    for i in range(groups * half):
        copy_out(i, mine, 0).wait()


def project(rows, columns, table, buffers):
    groups = len(columns)
    half, depth, width = columns[0].shape
    tokens = rows.shape[0]
    count = groups * half
    any_spec = pl.BlockSpec(memory_space=pl.ANY)
    vmem = pl.BlockSpec(memory_space=pltpu.VMEM)
    operands = [table, rows, *columns]
    in_specs = [pl.BlockSpec(memory_space=pltpu.SMEM), vmem] + [vmem] * groups
    aliases = {}
    if buffers is not None:
        operands += list(buffers)
        in_specs += [any_spec, any_spec]
        aliases = {2 + groups: 0, 3 + groups: 1}
    result = jax.ShapeDtypeStruct((SIDE, tokens, 2 * width), BF)
    return pl.pallas_call(
        functools.partial(project_kernel, groups, buffers is not None),
        out_shape=(result, result),
        in_specs=in_specs,
        out_specs=(any_spec, any_spec),
        scratch_shapes=[
            pltpu.VMEM((count, tokens, width), BF),
            pltpu.SemaphoreType.DMA((count,)),
        ],
        input_output_aliases=aliases,
        compiler_params=pltpu.CompilerParams(vmem_limit_bytes=24 * 1024 * 1024),
        cost_estimate=pl.CostEstimate(
            flops=2 * count * tokens * depth * width,
            bytes_accessed=2 * count * (depth * width + tokens * width),
            transcendentals=0,
        ),
        name="project",
    )(*operands)


def lift_kernel(count, steps, *refs):
    lefts, rights = refs[:count], refs[count : 2 * count]
    w_gate, w_up, hidden, gate, up = refs[2 * count :]
    i = pl.program_id(0)

    def step(xs, first):
        x = jnp.concatenate([r[...] for r in xs], axis=0)
        for w, total in ((w_gate, gate), (w_up, up)):
            part = lax.dot_general(
                x, w[...], (((1,), (1,)), ((), ())), preferred_element_type=F32
            )
            total[...] = part if first else total[...] + part

    @pl.when(i == 0)
    def _():
        step(lefts, True)

    @pl.when((i > 0) & (i < steps))
    def _():
        step(lefts, False)

    @pl.when(i >= steps)
    def _():
        step(rights, False)

    @pl.when(i == 2 * steps - 1)
    def _():
        g = gate[...]
        hidden[...] = (g / (1.0 + jnp.exp(-g)) * up[...]).astype(BF)


def lift(lefts, rights, w_gate, w_up):
    count = len(lefts)
    rows, half = lefts[0].shape
    units = w_gate.shape[0]
    tile = 1536
    steps = half // tile
    return pl.pallas_call(
        functools.partial(lift_kernel, count, steps),
        out_shape=jax.ShapeDtypeStruct((count * rows, units), BF),
        grid=(2 * steps,),
        in_specs=[pl.BlockSpec((rows, tile), lambda i: (0, jnp.minimum(i, steps - 1)))] * count
        + [pl.BlockSpec((rows, tile), lambda i: (0, jnp.maximum(i - steps, 0)))] * count
        + [pl.BlockSpec((units, tile), lambda i: (0, i))] * 2,
        out_specs=pl.BlockSpec((count * rows, units), lambda i: (0, 0)),
        scratch_shapes=[pltpu.VMEM((count * rows, units), F32)] * 2,
        compiler_params=pltpu.CompilerParams(vmem_limit_bytes=52 * 1024 * 1024),
        cost_estimate=pl.CostEstimate(
            flops=8 * count * rows * half * units,
            bytes_accessed=2 * (4 * half * units + count * rows * (2 * half + units)),
            transcendentals=count * rows * units,
        ),
        name="lift",
    )(*lefts, *rights, w_gate, w_up)


def lower_kernel(count, hidden, w_down, *outs):
    out = jnp.dot(hidden[...], w_down[...], preferred_element_type=F32).astype(BF)
    rows = out.shape[0] // count
    for n in range(count):
        outs[n][...] = out[n * rows : (n + 1) * rows]


def lower(hidden, w_down, count, side):
    units, model = w_down.shape
    rows = hidden.shape[0] // count
    tile = 1536
    steps = model // 2 // tile
    return pl.pallas_call(
        functools.partial(lower_kernel, count),
        out_shape=[jax.ShapeDtypeStruct((rows, model // 2), BF)] * count,
        grid=(steps,),
        in_specs=[
            pl.BlockSpec(hidden.shape, lambda i: (0, 0)),
            pl.BlockSpec((units, tile), lambda i: (0, side * steps + i)),
        ],
        out_specs=[pl.BlockSpec((rows, tile), lambda i: (0, i))] * count,
        compiler_params=pltpu.CompilerParams(vmem_limit_bytes=52 * 1024 * 1024),
        cost_estimate=pl.CostEstimate(
            flops=count * rows * model * units,
            bytes_accessed=model * units + count * rows * (model + 2 * units),
            transcendentals=0,
        ),
        name="lower",
    )(hidden, w_down)


def local_attention(queries, key_rows, values, log_decay):
    heads = log_decay.shape[0]
    length = queries.shape[0]
    shape = (length, heads, HEAD_DIM)
    q, k, v = (a.reshape(shape) for a in (queries, key_rows, values))
    later = lax.broadcasted_iota(jnp.int32, (length, length), 0)
    earlier = lax.broadcasted_iota(jnp.int32, (length, length), 1)
    causal = later >= earlier
    cumulative = jnp.cumsum(log_decay, axis=1)
    log_total = cumulative[:, -1]
    fall = jnp.exp(log_total[:, None] - cumulative).T
    keyed = (k.astype(F32) * fall[..., None]).astype(BF)
    update = jnp.einsum("shd,she->hde", keyed, v, preferred_element_type=F32)
    spread = cumulative[:, :, None] - cumulative[:, None, :]
    grid = jnp.where(causal, jnp.exp(jnp.where(causal, spread, 0.0)), 0.0)
    scores = jnp.einsum("thd,shd->hts", q, k, preferred_element_type=F32)
    weights = (scores * (grid * (1.0 / HEAD_DIM))).astype(BF)
    within = jnp.einsum("hts,shd->thd", weights, v, preferred_element_type=F32)
    return cumulative, log_total, update, within, q


def shards(
    queries, key_rows, values, log_decay, residual, w_out, w_gate, w_up, w_down, routes, gate_values
):
    length = queries.shape[0]
    heads = log_decay.shape[0]
    place, own = lax.axis_index("seq"), lax.axis_index("ep")
    z, y = place // SIDE, place % SIDE
    x, c = own // CORES, own % CORES
    pos_a = jnp.where(c == 0, y, z)
    pos_b = jnp.where(c == 0, z, y)

    w0, w1, w2, w3 = gather_pair(w_out, "a")
    w_top, w_bottom = jnp.stack([w0, w1]), jnp.stack([w2, w3])

    cumulative, log_total, update, within, q = local_attention(
        queries, key_rows, values, log_decay
    )
    state, messages, w_top, w_bottom = entering_state(log_total, update, z, y, w_top, w_bottom)
    g0, g1, g2, g3 = gather_halves(w_top, w_bottom, "b", messages)
    readout = jnp.einsum(
        "thd,hde->the", q.astype(F32), state, precision=lax.Precision.HIGHEST
    )
    carried = jnp.exp(cumulative).T[..., None] * readout * (1.0 / HEAD_DIM)
    attention = (within + carried).astype(BF).reshape(length, heads * HEAD_DIM)

    def table(offsets):
        a = (pos_a + jnp.array([o[0] for o in offsets])) % SIDE
        b = (pos_b + jnp.array([o[1] for o in offsets])) % SIDE
        j = jnp.where(c == 0, b * SIDE + a, a * SIDE + b)
        e = j // 2
        return ((((e % 2) != c) * SIDE + (e // 2 - x) % SIDE) * 2 + j % 2).astype(jnp.int32)

    everyone = lambda *bs: table([(a, b) for b in bs for a in range(SIDE)])
    partial = project(attention, g0, everyone(0), None)
    partial = project(attention, g1 + g3, everyone(1, 3), partial)
    partial = project(attention, g2, everyone(2), partial)

    other = send(partial[1], lambda pz, py, px, pc: (pz, py, px, pc + 1))
    both = [add(partial[0][d], other[d]) for d in range(SIDE)]
    arrived = [
        send(both[d].astype(BF), functools.partial(lambda d, pz, py, px, pc: (pz, py, px + d, pc), d))
        for d in range(1, SIDE)
    ]
    stream = add(residual, both[0], *arrived).astype(BF)

    experts = lax.axis_size("ep")
    capacity = length * 9 // (4 * experts)
    ids = jnp.arange(experts, dtype=jnp.int32)
    named = routes[None, :, :] == ids[:, None, None]
    is_named = jnp.any(named, axis=2)
    rank = jnp.cumsum(is_named.astype(jnp.int32), axis=1) - 1
    slots = jnp.arange(capacity, dtype=jnp.int32)
    chosen = is_named[:, None, :] & (rank[:, None, :] == slots[None, :, None])
    weight = jnp.sum(jnp.where(named, gate_values[None], 0.0), axis=2)

    width = stream.shape[1]
    wide = stream.astype(F32)
    squares = jnp.sum(wide * wide, axis=1, keepdims=True)
    s0 = squares.astype(BF).astype(F32)
    s1 = (squares - s0).astype(BF).astype(F32)
    s2 = squares - s0 - s1
    lane = lax.broadcasted_iota(jnp.int32, (length, 128), 1)
    tail = jnp.where(lane == 0, s0, jnp.where(lane == 1, s1, jnp.where(lane == 2, s2, 0.0)))
    rows = jnp.concatenate([stream, tail.astype(BF)], axis=1)
    picked = jnp.dot(
        chosen.astype(BF).reshape(experts * capacity, length), rows, preferred_element_type=F32
    ).astype(BF)
    got = lax.all_to_all(picked.reshape(experts, capacity, width + 128), "ep", 0, 0)
    square_sum = jnp.sum(got[:, :, width : width + 3].astype(F32), axis=(0, 2))
    scale = lax.rsqrt(square_sum / (experts * width) + EPSILON)
    normed = (got[:, :, :width].astype(F32) * scale[None, :, None]).astype(BF)
    packed = jnp.transpose(normed, (1, 0, 2)).reshape(capacity, experts * width)

    half = packed.shape[1] // 2
    c1, c3 = shift(packed, "a", -1, "pair_1"), shift(packed, "a", 1, "pair_3")
    halves = lambda m, n: [
        jnp.concatenate([p[:, i * half : (i + 1) * half] for p in (m, n)], axis=0) for i in range(2)
    ]
    odd_l, odd_r, _ = ring_rows(*halves(c1, c3), "odd")
    c2l = shift(c1[:, :half], "a", -1, "pair_2_left")
    c2r = shift(c3[:, half:], "a", 1, "pair_2_right")
    even_own = [
        jnp.concatenate([packed[:, :half], c2l], axis=0),
        jnp.concatenate([packed[:, half:], c2r], axis=0),
    ]
    even_own, _ = lax.optimization_barrier((even_own, (odd_l[1], odd_r[3])))
    gate_rows, up_rows, down = w_gate[0].T, w_up[0].T, w_down[0]
    hidden_odd = lift(odd_l, odd_r, gate_rows, up_rows)
    even_l, even_r, hidden_odd = ring_rows(*even_own, "even", hidden_odd)
    hidden_even = lift(even_l, even_r, gate_rows, up_rows)
    part_l, part_r = (lower(hidden_odd, down, SIDE, side) for side in range(2))
    sum_odd_l, sum_odd_r, hidden_even = ring_sums(part_l, part_r, "back_odd", hidden_even)
    part_l, part_r = (lower(hidden_even, down, SIDE, side) for side in range(2))
    sum_even_l, sum_even_r, _ = ring_sums(part_l, part_r, "back_even")
    mine = []
    for odd, even, n in ((sum_odd_l, sum_even_l, "left"), (sum_odd_r, sum_even_r, "right")):
        mine.append(
            add(
                even[:capacity],
                shift(even[capacity:].astype(BF), "a", 2, "back_pair_2_" + n),
                shift(odd[:capacity].astype(BF), "a", 1, "back_pair_1_" + n),
                shift(odd[capacity:].astype(BF), "a", -1, "back_pair_3_" + n),
            ).astype(BF)
        )

    returned = lax.all_to_all(
        jnp.concatenate(
            [jnp.transpose(m.reshape(capacity, experts // 2, width), (1, 0, 2)) for m in mine], axis=0
        ),
        "ep",
        0,
        0,
    )
    w_hi = weight.astype(BF).astype(F32)
    w_lo = weight - w_hi
    spread = jnp.concatenate(
        [jnp.where(chosen, w[:, None, :], 0.0).astype(BF) for w in (w_hi, w_lo)], axis=0
    ).reshape(2 * experts * capacity, length)
    flat = returned.reshape(experts * capacity, width)
    mix = lax.dot_general(
        spread,
        jnp.concatenate([flat, flat], axis=0),
        (((0,), (0,)), ((), ())),
        preferred_element_type=F32,
    )
    return attention, mix.astype(BF)


def solution(mesh):
    placed = (
        P("seq", "ep"),
        P("seq", "ep"),
        P("seq", "ep"),
        P("ep", "seq"),
        P("seq", "ep"),
        P("ep", "seq"),
        P("ep", None, "seq"),
        P("ep", None, "seq"),
        P("ep", "seq", None),
        P("seq", None),
        P("seq", None),
    )
    return jax.shard_map(
        shards,
        mesh=mesh,
        in_specs=placed,
        out_specs=(P("seq", "ep"), P("seq", "ep")),
        check_vma=False,
    )
```

```python
import functools

import jax
import jax.numpy as jnp
from jax import lax
from jax.experimental import pallas as pl
from jax.experimental.pallas import tpu as pltpu
from jax.sharding import PartitionSpec as P

HEAD_DIM = 128
EPSILON = 1e-06
SIDE = 4
CORES = 2
BF = jnp.bfloat16
F32 = jnp.float32


def pairs(move):
    out = []
    for z in range(SIDE):
        for y in range(SIDE):
            for x in range(SIDE):
                for c in range(CORES):
                    source = ((z * SIDE + y) * SIDE + x) * CORES + c
                    place = move(z, y, x, c)
                    if place is None:
                        continue
                    tz, ty, tx, tc = place
                    tz, ty, tx, tc = tz % SIDE, ty % SIDE, tx % SIDE, tc % CORES
                    out.append((source, ((tz * SIDE + ty) * SIDE + tx) * CORES + tc))
    return out


def send(value, move):
    return lax.ppermute(value, ("seq", "ep"), pairs(move))


def shift(value, axis, d, name="block"):
    def move(z, y, x, c):
        if (axis == "a") == (c == 0):
            return z, y + d, x, c
        return z + d, y, x, c

    with jax.named_scope(name):
        return send(value, move)


def gather_pair(block, axis):
    far = shift(block, axis, 2, "pair_2")
    return block, shift(block, axis, -1, "pair_1"), far, shift(block, axis, 1, "pair_3")


def gather_halves(top, bottom, axis, after=None):
    top_1, bottom_3 = shift(top, axis, -1, "top_1"), shift(bottom, axis, 1, "bottom_3")
    if after is not None:
        top, bottom, _ = lax.optimization_barrier((top, bottom, after))
    bottom_1, top_3 = shift(bottom, axis, -1, "bottom_1"), shift(top, axis, 1, "top_3")
    top_2 = shift(top_1, axis, -1, "top_2")
    bottom_2 = shift(bottom_3, axis, 1, "bottom_2")
    return (top, bottom), (top_1, bottom_1), (top_2, bottom_2), (top_3, bottom_3)


def exchange(blocks):
    got = {0: blocks[0]}
    for k in (2, 6, 1, 5, 3, 7, 4):
        with jax.named_scope("over_ep"):
            got[k] = send(
                blocks[k],
                functools.partial(
                    lambda dx, dc, pz, py, px, pc: (pz, py, px + dx, pc + dc), k % SIDE, k // SIDE
                ),
            )
    return [got[k] for k in range(2 * SIDE)]


def ring_rows(left, right, name, beside=None):
    left_1, right_3 = shift(left, "b", -1, name + "_left_1"), shift(right, "b", 1, name + "_right_3")
    right_1, left_3 = shift(right, "b", -1, name + "_right_1"), shift(left, "b", 1, name + "_left_3")
    if beside is not None:
        left_1, right_3, beside = lax.optimization_barrier((left_1, right_3, beside))
    left_2 = shift(left_1, "b", -1, name + "_left_2")
    right_2 = shift(right_3, "b", 1, name + "_right_2")
    return [left, left_1, left_2, left_3], [right, right_1, right_2, right_3], beside


def ring_sums(lefts, rights, name, beside=None):
    from_2l, far_3 = shift(lefts[2], "b", 1, name + "_left_2"), shift(lefts[3], "b", -1, name + "_left_3")
    from_2r, far_1 = shift(rights[2], "b", -1, name + "_right_2"), shift(rights[1], "b", 1, name + "_right_1")
    if beside is not None:
        from_2l, from_2r, beside = lax.optimization_barrier((from_2l, from_2r, beside))
    near_1 = shift(add(lefts[1], from_2l).astype(BF), "b", 1, name + "_left_1")
    near_3 = shift(add(rights[3], from_2r).astype(BF), "b", -1, name + "_right_3")
    return add(lefts[0], far_3, near_1), add(rights[0], far_1, near_3), beside


def add(*parts):
    return functools.reduce(lambda a, b: a + b, [p.astype(F32) for p in parts])


def line_state(log_total, state, move_of):
    rows = state.reshape(-1, HEAD_DIM).astype(BF)
    high = log_total.astype(BF)
    mid = (log_total - high.astype(F32)).astype(BF)
    low = (log_total - high.astype(F32) - mid.astype(F32)).astype(BF)
    heads = log_total.shape[0]
    extra = jnp.zeros((16, HEAD_DIM), BF)
    extra = extra.at[0, :heads].set(high).at[1, :heads].set(mid).at[2, :heads].set(low)
    message = jnp.concatenate([rows, extra], axis=0)
    got = [send(message, move_of(d)) for d in range(1, SIDE)]

    def parse(m):
        t = m[-16:-13, :heads].astype(F32).sum(axis=0)
        return t, m[:-16].astype(F32).reshape(state.shape)

    return [(log_total, state)] + [parse(m) for m in got], got


def chain(earlier, later):
    return (
        earlier[0] + later[0],
        jnp.exp(later[0])[:, None, None] * earlier[1] + later[1],
    )


def entering_state(log_total, state, z, y, w_top, w_bottom):
    line, _ = line_state(
        log_total, state, lambda d: lambda pz, py, px, pc: (pz, py + d, px, pc)
    )

    def masked(part, keep):
        return jnp.where(keep, part[0], 0.0), jnp.where(keep, part[1], 0.0)

    def prefix(parts, place):
        total = (jnp.zeros_like(log_total), jnp.zeros_like(state))
        for d in range(SIDE - 1, 0, -1):
            total = chain(total, masked(parts[d], d <= place))
        return total

    before_y = prefix(line, y)
    after = (jnp.zeros_like(log_total), jnp.zeros_like(state))
    for d in range(SIDE - 1, 0, -1):
        after = chain(after, masked(line[d], d > y))
    whole = chain(chain(before_y, line[0]), after)
    whole, w_top, w_bottom = lax.optimization_barrier((whole, w_top, w_bottom))
    lines, messages = line_state(
        whole[0], whole[1], lambda d: lambda pz, py, px, pc: (pz + d, py, px, pc)
    )
    before_z = prefix(lines, z)
    return chain(before_z, before_y)[1], messages, w_top, w_bottom


def project_kernel(groups, has_buffer, table, rows, *rest):
    columns = rest[:groups]
    mine, other, product, sems = rest[-4:]
    half, width = product.shape[0] // groups, product.shape[2]
    experts = mine.shape[0]

    def copy_out(i, dest, t):
        place = dest.at[t // 2, :, pl.ds(pl.multiple_of((t % 2) * width, 128), width)]
        return pltpu.make_async_copy(product.at[i], place, sems.at[i])

    for i in range(groups * half):
        product[i] = jnp.dot(
            rows[...], columns[i // half][i % half], preferred_element_type=F32
        ).astype(BF)
        t = table[i]

        @pl.when(t < 2 * experts)
        def _():
            copy_out(i, mine, t).start()

        @pl.when(t >= 2 * experts)
        def _():
            copy_out(i, other, t - 2 * experts).start()

    for i in range(groups * half):
        copy_out(i, mine, 0).wait()


def project(rows, columns, table, buffers):
    groups = len(columns)
    half, depth, width = columns[0].shape
    tokens = rows.shape[0]
    count = groups * half
    any_spec = pl.BlockSpec(memory_space=pl.ANY)
    vmem = pl.BlockSpec(memory_space=pltpu.VMEM)
    operands = [table, rows, *columns]
    in_specs = [pl.BlockSpec(memory_space=pltpu.SMEM), vmem] + [vmem] * groups
    aliases = {}
    if buffers is not None:
        operands += list(buffers)
        in_specs += [any_spec, any_spec]
        aliases = {2 + groups: 0, 3 + groups: 1}
    result = jax.ShapeDtypeStruct((SIDE, tokens, 2 * width), BF)
    return pl.pallas_call(
        functools.partial(project_kernel, groups, buffers is not None),
        out_shape=(result, result),
        in_specs=in_specs,
        out_specs=(any_spec, any_spec),
        scratch_shapes=[
            pltpu.VMEM((count, tokens, width), BF),
            pltpu.SemaphoreType.DMA((count,)),
        ],
        input_output_aliases=aliases,
        compiler_params=pltpu.CompilerParams(vmem_limit_bytes=24 * 1024 * 1024),
        cost_estimate=pl.CostEstimate(
            flops=2 * count * tokens * depth * width,
            bytes_accessed=2 * count * (depth * width + tokens * width),
            transcendentals=0,
        ),
        name="project",
    )(*operands)


def lift_kernel(count, steps, *refs):
    lefts, rights = refs[:count], refs[count : 2 * count]
    w_gate, w_up, hidden, gate, up = refs[2 * count :]
    i = pl.program_id(0)

    def step(xs, first):
        x = jnp.concatenate([r[...] for r in xs], axis=0)
        for w, total in ((w_gate, gate), (w_up, up)):
            part = lax.dot_general(
                x, w[...], (((1,), (1,)), ((), ())), preferred_element_type=F32
            )
            total[...] = part if first else total[...] + part

    @pl.when(i == 0)
    def _():
        step(lefts, True)

    @pl.when((i > 0) & (i < steps))
    def _():
        step(lefts, False)

    @pl.when(i >= steps)
    def _():
        step(rights, False)

    @pl.when(i == 2 * steps - 1)
    def _():
        g = gate[...]
        hidden[...] = (g / (1.0 + jnp.exp(-g)) * up[...]).astype(BF)


def lift(lefts, rights, w_gate, w_up):
    count = len(lefts)
    rows, half = lefts[0].shape
    units = w_gate.shape[0]
    tile = 1536
    steps = half // tile
    return pl.pallas_call(
        functools.partial(lift_kernel, count, steps),
        out_shape=jax.ShapeDtypeStruct((count * rows, units), BF),
        grid=(2 * steps,),
        in_specs=[pl.BlockSpec((rows, tile), lambda i: (0, jnp.minimum(i, steps - 1)))] * count
        + [pl.BlockSpec((rows, tile), lambda i: (0, jnp.maximum(i - steps, 0)))] * count
        + [pl.BlockSpec((units, tile), lambda i: (0, i))] * 2,
        out_specs=pl.BlockSpec((count * rows, units), lambda i: (0, 0)),
        scratch_shapes=[pltpu.VMEM((count * rows, units), F32)] * 2,
        compiler_params=pltpu.CompilerParams(vmem_limit_bytes=52 * 1024 * 1024),
        cost_estimate=pl.CostEstimate(
            flops=8 * count * rows * half * units,
            bytes_accessed=2 * (4 * half * units + count * rows * (2 * half + units)),
            transcendentals=count * rows * units,
        ),
        name="lift",
    )(*lefts, *rights, w_gate, w_up)


def lower_kernel(count, hidden, w_down, *outs):
    out = jnp.dot(hidden[...], w_down[...], preferred_element_type=F32).astype(BF)
    rows = out.shape[0] // count
    for n in range(count):
        outs[n][...] = out[n * rows : (n + 1) * rows]


def lower(hidden, w_down, count, side):
    units, model = w_down.shape
    rows = hidden.shape[0] // count
    tile = 1536
    steps = model // 2 // tile
    return pl.pallas_call(
        functools.partial(lower_kernel, count),
        out_shape=[jax.ShapeDtypeStruct((rows, model // 2), BF)] * count,
        grid=(steps,),
        in_specs=[
            pl.BlockSpec(hidden.shape, lambda i: (0, 0)),
            pl.BlockSpec((units, tile), lambda i: (0, side * steps + i)),
        ],
        out_specs=[pl.BlockSpec((rows, tile), lambda i: (0, i))] * count,
        compiler_params=pltpu.CompilerParams(vmem_limit_bytes=52 * 1024 * 1024),
        cost_estimate=pl.CostEstimate(
            flops=count * rows * model * units,
            bytes_accessed=model * units + count * rows * (model + 2 * units),
            transcendentals=0,
        ),
        name="lower",
    )(hidden, w_down)


def local_attention(queries, key_rows, values, log_decay):
    heads = log_decay.shape[0]
    length = queries.shape[0]
    shape = (length, heads, HEAD_DIM)
    q, k, v = (a.reshape(shape) for a in (queries, key_rows, values))
    later = lax.broadcasted_iota(jnp.int32, (length, length), 0)
    earlier = lax.broadcasted_iota(jnp.int32, (length, length), 1)
    causal = later >= earlier
    cumulative = jnp.cumsum(log_decay, axis=1)
    log_total = cumulative[:, -1]
    fall = jnp.exp(log_total[:, None] - cumulative).T
    keyed = (k.astype(F32) * fall[..., None]).astype(BF)
    update = jnp.einsum("shd,she->hde", keyed, v, preferred_element_type=F32)
    spread = cumulative[:, :, None] - cumulative[:, None, :]
    grid = jnp.where(causal, jnp.exp(jnp.where(causal, spread, 0.0)), 0.0)
    scores = jnp.einsum("thd,shd->hts", q, k, preferred_element_type=F32)
    weights = (scores * (grid * (1.0 / HEAD_DIM))).astype(BF)
    within = jnp.einsum("hts,shd->thd", weights, v, preferred_element_type=F32)
    return cumulative, log_total, update, within, q


def shards(
    queries, key_rows, values, log_decay, residual, w_out, w_gate, w_up, w_down, routes, gate_values
):
    length = queries.shape[0]
    heads = log_decay.shape[0]
    place, own = lax.axis_index("seq"), lax.axis_index("ep")
    z, y = place // SIDE, place % SIDE
    x, c = own // CORES, own % CORES
    pos_a = jnp.where(c == 0, y, z)
    pos_b = jnp.where(c == 0, z, y)

    w0, w1, w2, w3 = gather_pair(w_out, "a")
    w_top, w_bottom = jnp.stack([w0, w1]), jnp.stack([w2, w3])

    cumulative, log_total, update, within, q = local_attention(
        queries, key_rows, values, log_decay
    )
    state, messages, w_top, w_bottom = entering_state(log_total, update, z, y, w_top, w_bottom)
    g0, g1, g2, g3 = gather_halves(w_top, w_bottom, "b", messages)
    readout = jnp.einsum(
        "thd,hde->the", q.astype(F32), state, precision=lax.Precision.HIGHEST
    )
    carried = jnp.exp(cumulative).T[..., None] * readout * (1.0 / HEAD_DIM)
    attention = (within + carried).astype(BF).reshape(length, heads * HEAD_DIM)

    experts = lax.axis_size("ep")
    capacity = length * 9 // (4 * experts)
    steps = jnp.arange(experts, dtype=jnp.int32)
    slots = jnp.arange(capacity, dtype=jnp.int32)

    def places(ids):
        named = routes[None, :, :] == ids[:, None, None]
        is_named = jnp.any(named, axis=2)
        rank = jnp.cumsum(is_named.astype(jnp.int32), axis=1) - 1
        chosen = is_named[:, None, :] & (rank[:, None, :] == slots[None, :, None])
        return chosen, jnp.sum(jnp.where(named, gate_values[None], 0.0), axis=2)

    chosen, weight = places(steps)
    picks = places((x + steps % SIDE) % SIDE * CORES + (c + steps // SIDE) % CORES)[0].astype(BF)
    attention, picks = lax.optimization_barrier((attention, picks))

    def table(offsets):
        a = (pos_a + jnp.array([o[0] for o in offsets])) % SIDE
        b = (pos_b + jnp.array([o[1] for o in offsets])) % SIDE
        j = jnp.where(c == 0, b * SIDE + a, a * SIDE + b)
        e = j // 2
        return ((((e % 2) != c) * SIDE + (e // 2 - x) % SIDE) * 2 + j % 2).astype(jnp.int32)

    everyone = lambda *bs: table([(a, b) for b in bs for a in range(SIDE)])
    partial = project(attention, g0, everyone(0), None)
    partial = project(attention, g1 + g3, everyone(1, 3), partial)
    partial = project(attention, g2, everyone(2), partial)

    other = send(partial[1], lambda pz, py, px, pc: (pz, py, px, pc + 1))
    both = [add(partial[0][d], other[d]) for d in range(SIDE)]
    arrived = [
        send(both[d].astype(BF), functools.partial(lambda d, pz, py, px, pc: (pz, py, px + d, pc), d))
        for d in range(1, SIDE)
    ]
    stream = add(residual, both[0], *arrived).astype(BF)

    width = stream.shape[1]
    wide = stream.astype(F32)
    squares = jnp.sum(wide * wide, axis=1, keepdims=True)
    s0 = squares.astype(BF).astype(F32)
    s1 = (squares - s0).astype(BF).astype(F32)
    s2 = squares - s0 - s1
    lane = lax.broadcasted_iota(jnp.int32, (length, 128), 1)
    tail = jnp.where(lane == 0, s0, jnp.where(lane == 1, s1, jnp.where(lane == 2, s2, 0.0)))
    rows = jnp.concatenate([stream, tail.astype(BF)], axis=1)
    picked = jnp.dot(
        picks.reshape(experts * capacity, length), rows, preferred_element_type=F32
    ).astype(BF)
    picked = picked.reshape(experts, capacity, width + 128)
    got = jnp.stack(exchange([picked[k] for k in range(experts)]))
    square_sum = jnp.sum(got[:, :, width : width + 3].astype(F32), axis=(0, 2))
    scale = lax.rsqrt(square_sum / (experts * width) + EPSILON)
    place_of = (steps - c) % CORES * SIDE + (x - steps // CORES) % SIDE
    normed = (got[:, :, :width].astype(F32) * scale[None, :, None]).astype(BF)
    packed = jnp.transpose(normed[place_of], (1, 0, 2)).reshape(capacity, experts * width)

    half = packed.shape[1] // 2
    c1, c3 = shift(packed, "a", -1, "pair_1"), shift(packed, "a", 1, "pair_3")
    halves = lambda m, n: [
        jnp.concatenate([p[:, i * half : (i + 1) * half] for p in (m, n)], axis=0) for i in range(2)
    ]
    odd_l, odd_r, _ = ring_rows(*halves(c1, c3), "odd")
    c2l = shift(c1[:, :half], "a", -1, "pair_2_left")
    c2r = shift(c3[:, half:], "a", 1, "pair_2_right")
    even_own = [
        jnp.concatenate([packed[:, :half], c2l], axis=0),
        jnp.concatenate([packed[:, half:], c2r], axis=0),
    ]
    even_own, _ = lax.optimization_barrier((even_own, (odd_l[1], odd_r[3])))
    gate_rows, up_rows, down = w_gate[0].T, w_up[0].T, w_down[0]
    hidden_odd = lift(odd_l, odd_r, gate_rows, up_rows)
    even_l, even_r, hidden_odd = ring_rows(*even_own, "even", hidden_odd)
    hidden_even = lift(even_l, even_r, gate_rows, up_rows)
    part_l, part_r = (lower(hidden_odd, down, SIDE, side) for side in range(2))
    sum_odd_l, sum_odd_r, hidden_even = ring_sums(part_l, part_r, "back_odd", hidden_even)
    part_l, part_r = (lower(hidden_even, down, SIDE, side) for side in range(2))
    sum_even_l, sum_even_r, _ = ring_sums(part_l, part_r, "back_even")
    mine = []
    for odd, even, n in ((sum_odd_l, sum_even_l, "left"), (sum_odd_r, sum_even_r, "right")):
        mine.append(
            add(
                even[:capacity],
                shift(even[capacity:].astype(BF), "a", 2, "back_pair_2_" + n),
                shift(odd[:capacity].astype(BF), "a", 1, "back_pair_1_" + n),
                shift(odd[capacity:].astype(BF), "a", -1, "back_pair_3_" + n),
            ).astype(BF)
        )

    returned = lax.all_to_all(
        jnp.concatenate(
            [jnp.transpose(m.reshape(capacity, experts // 2, width), (1, 0, 2)) for m in mine], axis=0
        ),
        "ep",
        0,
        0,
    )
    w_hi = weight.astype(BF).astype(F32)
    w_lo = weight - w_hi
    spread = jnp.concatenate(
        [jnp.where(chosen, w[:, None, :], 0.0).astype(BF) for w in (w_hi, w_lo)], axis=0
    ).reshape(2 * experts * capacity, length)
    flat = returned.reshape(experts * capacity, width)
    mix = lax.dot_general(
        spread,
        jnp.concatenate([flat, flat], axis=0),
        (((0,), (0,)), ((), ())),
        preferred_element_type=F32,
    )
    return attention, mix.astype(BF)


def solution(mesh):
    placed = (
        P("seq", "ep"),
        P("seq", "ep"),
        P("seq", "ep"),
        P("ep", "seq"),
        P("seq", "ep"),
        P("ep", "seq"),
        P("ep", None, "seq"),
        P("ep", None, "seq"),
        P("ep", "seq", None),
        P("seq", None),
        P("seq", None),
    )
    return jax.shard_map(
        shards,
        mesh=mesh,
        in_specs=placed,
        out_specs=(P("seq", "ep"), P("seq", "ep")),
        check_vma=False,
    )
```

```python
import functools

import jax
import jax.numpy as jnp
from jax import lax
from jax.experimental import pallas as pl
from jax.experimental.pallas import tpu as pltpu
from jax.sharding import PartitionSpec as P

HEAD_DIM = 128
EPSILON = 1e-06
SIDE = 4
CORES = 2
BF = jnp.bfloat16
F32 = jnp.float32


def pairs(move):
    out = []
    for z in range(SIDE):
        for y in range(SIDE):
            for x in range(SIDE):
                for c in range(CORES):
                    source = ((z * SIDE + y) * SIDE + x) * CORES + c
                    place = move(z, y, x, c)
                    if place is None:
                        continue
                    tz, ty, tx, tc = place
                    tz, ty, tx, tc = tz % SIDE, ty % SIDE, tx % SIDE, tc % CORES
                    out.append((source, ((tz * SIDE + ty) * SIDE + tx) * CORES + tc))
    return out


def send(value, move):
    return lax.ppermute(value, ("seq", "ep"), pairs(move))


def shift(value, axis, d, name="block"):
    def move(z, y, x, c):
        if (axis == "a") == (c == 0):
            return z, y + d, x, c
        return z + d, y, x, c

    with jax.named_scope(name):
        return send(value, move)


def gather_halves(top, bottom, axis, after=None):
    top_1, bottom_3 = shift(top, axis, -1, "top_1"), shift(bottom, axis, 1, "bottom_3")
    if after is not None:
        top, bottom, _ = lax.optimization_barrier((top, bottom, after))
    bottom_1, top_3 = shift(bottom, axis, -1, "bottom_1"), shift(top, axis, 1, "top_3")
    top_2 = shift(top_1, axis, -1, "top_2")
    bottom_2 = shift(bottom_3, axis, 1, "bottom_2")
    return (top, bottom), (top_1, bottom_1), (top_2, bottom_2), (top_3, bottom_3)


def exchange(blocks):
    got = {0: blocks[0]}
    for k in (2, 6, 1, 5, 3, 7, 4):
        with jax.named_scope("over_ep"):
            got[k] = send(
                blocks[k],
                functools.partial(
                    lambda dx, dc, pz, py, px, pc: (pz, py, px + dx, pc + dc), k % SIDE, k // SIDE
                ),
            )
    return [got[k] for k in range(2 * SIDE)]


def ring_rows(left, right, name, beside=None):
    left_1, right_3 = shift(left, "b", -1, name + "_left_1"), shift(right, "b", 1, name + "_right_3")
    right_1, left_3 = shift(right, "b", -1, name + "_right_1"), shift(left, "b", 1, name + "_left_3")
    if beside is not None:
        left_1, right_3, beside = lax.optimization_barrier((left_1, right_3, beside))
    left_2 = shift(left_1, "b", -1, name + "_left_2")
    right_2 = shift(right_3, "b", 1, name + "_right_2")
    return [left, left_1, left_2, left_3], [right, right_1, right_2, right_3], beside


def ring_sums(lefts, rights, name, beside=None):
    from_2l, far_3 = shift(lefts[2], "b", 1, name + "_left_2"), shift(lefts[3], "b", -1, name + "_left_3")
    from_2r, far_1 = shift(rights[2], "b", -1, name + "_right_2"), shift(rights[1], "b", 1, name + "_right_1")
    if beside is not None:
        from_2l, from_2r, beside = lax.optimization_barrier((from_2l, from_2r, beside))
    near_1 = shift(add(lefts[1], from_2l).astype(BF), "b", 1, name + "_left_1")
    near_3 = shift(add(rights[3], from_2r).astype(BF), "b", -1, name + "_right_3")
    return add(lefts[0], far_3, near_1), add(rights[0], far_1, near_3), beside


def add(*parts):
    return functools.reduce(lambda a, b: a + b, [p.astype(F32) for p in parts])


def line_state(log_total, state, move_of):
    rows = state.reshape(-1, HEAD_DIM).astype(BF)
    high = log_total.astype(BF)
    mid = (log_total - high.astype(F32)).astype(BF)
    low = (log_total - high.astype(F32) - mid.astype(F32)).astype(BF)
    heads = log_total.shape[0]
    extra = jnp.zeros((16, HEAD_DIM), BF)
    extra = extra.at[0, :heads].set(high).at[1, :heads].set(mid).at[2, :heads].set(low)
    message = jnp.concatenate([rows, extra], axis=0)
    got = [send(message, move_of(d)) for d in range(1, SIDE)]

    def parse(m):
        t = m[-16:-13, :heads].astype(F32).sum(axis=0)
        return t, m[:-16].astype(F32).reshape(state.shape)

    return [(log_total, state)] + [parse(m) for m in got], got


def chain(earlier, later):
    return (
        earlier[0] + later[0],
        jnp.exp(later[0])[:, None, None] * earlier[1] + later[1],
    )


def entering_state(log_total, state, z, y, beside, behind):
    line, messages = line_state(
        log_total, state, lambda d: lambda pz, py, px, pc: (pz, py + d, px, pc)
    )
    behind, _ = lax.optimization_barrier((behind, messages))

    def masked(part, keep):
        return jnp.where(keep, part[0], 0.0), jnp.where(keep, part[1], 0.0)

    def prefix(parts, place):
        total = (jnp.zeros_like(log_total), jnp.zeros_like(state))
        for d in range(SIDE - 1, 0, -1):
            total = chain(total, masked(parts[d], d <= place))
        return total

    before_y = prefix(line, y)
    after = (jnp.zeros_like(log_total), jnp.zeros_like(state))
    for d in range(SIDE - 1, 0, -1):
        after = chain(after, masked(line[d], d > y))
    whole = chain(chain(before_y, line[0]), after)
    whole, beside = lax.optimization_barrier((whole, beside))
    lines, messages = line_state(
        whole[0], whole[1], lambda d: lambda pz, py, px, pc: (pz + d, py, px, pc)
    )
    before_z = prefix(lines, z)
    return chain(before_z, before_y)[1], messages, beside, behind


def project_kernel(groups, has_buffer, table, rows, *rest):
    columns = rest[:groups]
    mine, other, product, sems = rest[-4:]
    half, width = product.shape[0] // groups, product.shape[2]
    experts = mine.shape[0]

    def copy_out(i, dest, t):
        place = dest.at[t // 2, :, pl.ds(pl.multiple_of((t % 2) * width, 128), width)]
        return pltpu.make_async_copy(product.at[i], place, sems.at[i])

    for i in range(groups * half):
        product[i] = jnp.dot(
            rows[...], columns[i // half][i % half], preferred_element_type=F32
        ).astype(BF)
        t = table[i]

        @pl.when(t < 2 * experts)
        def _():
            copy_out(i, mine, t).start()

        @pl.when(t >= 2 * experts)
        def _():
            copy_out(i, other, t - 2 * experts).start()

    for i in range(groups * half):
        copy_out(i, mine, 0).wait()


def project(rows, columns, table, buffers):
    groups = len(columns)
    half, depth, width = columns[0].shape
    tokens = rows.shape[0]
    count = groups * half
    any_spec = pl.BlockSpec(memory_space=pl.ANY)
    vmem = pl.BlockSpec(memory_space=pltpu.VMEM)
    operands = [table, rows, *columns]
    in_specs = [pl.BlockSpec(memory_space=pltpu.SMEM), vmem] + [vmem] * groups
    aliases = {}
    if buffers is not None:
        operands += list(buffers)
        in_specs += [any_spec, any_spec]
        aliases = {2 + groups: 0, 3 + groups: 1}
    result = jax.ShapeDtypeStruct((SIDE, tokens, 2 * width), BF)
    return pl.pallas_call(
        functools.partial(project_kernel, groups, buffers is not None),
        out_shape=(result, result),
        in_specs=in_specs,
        out_specs=(any_spec, any_spec),
        scratch_shapes=[
            pltpu.VMEM((count, tokens, width), BF),
            pltpu.SemaphoreType.DMA((count,)),
        ],
        input_output_aliases=aliases,
        compiler_params=pltpu.CompilerParams(vmem_limit_bytes=24 * 1024 * 1024),
        cost_estimate=pl.CostEstimate(
            flops=2 * count * tokens * depth * width,
            bytes_accessed=2 * count * (depth * width + tokens * width),
            transcendentals=0,
        ),
        name="project",
    )(*operands)


def lift_kernel(count, steps, *refs):
    lefts, rights = refs[:count], refs[count : 2 * count]
    w_gate, w_up, hidden, gate, up = refs[2 * count :]
    i = pl.program_id(0)

    def step(xs, first):
        x = jnp.concatenate([r[...] for r in xs], axis=0)
        for w, total in ((w_gate, gate), (w_up, up)):
            part = lax.dot_general(
                x, w[...], (((1,), (1,)), ((), ())), preferred_element_type=F32
            )
            total[...] = part if first else total[...] + part

    @pl.when(i == 0)
    def _():
        step(lefts, True)

    @pl.when((i > 0) & (i < steps))
    def _():
        step(lefts, False)

    @pl.when(i >= steps)
    def _():
        step(rights, False)

    @pl.when(i == 2 * steps - 1)
    def _():
        g = gate[...]
        hidden[...] = (g / (1.0 + jnp.exp(-g)) * up[...]).astype(BF)


def lift(lefts, rights, w_gate, w_up):
    count = len(lefts)
    rows, half = lefts[0].shape
    units = w_gate.shape[0]
    tile = 1536
    steps = half // tile
    return pl.pallas_call(
        functools.partial(lift_kernel, count, steps),
        out_shape=jax.ShapeDtypeStruct((count * rows, units), BF),
        grid=(2 * steps,),
        in_specs=[pl.BlockSpec((rows, tile), lambda i: (0, jnp.minimum(i, steps - 1)))] * count
        + [pl.BlockSpec((rows, tile), lambda i: (0, jnp.maximum(i - steps, 0)))] * count
        + [pl.BlockSpec((units, tile), lambda i: (0, i))] * 2,
        out_specs=pl.BlockSpec((count * rows, units), lambda i: (0, 0)),
        scratch_shapes=[pltpu.VMEM((count * rows, units), F32)] * 2,
        compiler_params=pltpu.CompilerParams(vmem_limit_bytes=52 * 1024 * 1024),
        cost_estimate=pl.CostEstimate(
            flops=8 * count * rows * half * units,
            bytes_accessed=2 * (4 * half * units + count * rows * (2 * half + units)),
            transcendentals=count * rows * units,
        ),
        name="lift",
    )(*lefts, *rights, w_gate, w_up)


def lower_kernel(count, hidden, w_down, *outs):
    out = jnp.dot(hidden[...], w_down[...], preferred_element_type=F32).astype(BF)
    rows = out.shape[0] // count
    for n in range(count):
        outs[n][...] = out[n * rows : (n + 1) * rows]


def lower(hidden, w_down, count, side):
    units, model = w_down.shape
    rows = hidden.shape[0] // count
    tile = 1536
    steps = model // 2 // tile
    return pl.pallas_call(
        functools.partial(lower_kernel, count),
        out_shape=[jax.ShapeDtypeStruct((rows, model // 2), BF)] * count,
        grid=(steps,),
        in_specs=[
            pl.BlockSpec(hidden.shape, lambda i: (0, 0)),
            pl.BlockSpec((units, tile), lambda i: (0, side * steps + i)),
        ],
        out_specs=[pl.BlockSpec((rows, tile), lambda i: (0, i))] * count,
        compiler_params=pltpu.CompilerParams(vmem_limit_bytes=52 * 1024 * 1024),
        cost_estimate=pl.CostEstimate(
            flops=count * rows * model * units,
            bytes_accessed=model * units + count * rows * (model + 2 * units),
            transcendentals=0,
        ),
        name="lower",
    )(hidden, w_down)


def local_attention(queries, key_rows, values, log_decay):
    heads = log_decay.shape[0]
    length = queries.shape[0]
    shape = (length, heads, HEAD_DIM)
    q, k, v = (a.reshape(shape) for a in (queries, key_rows, values))
    later = lax.broadcasted_iota(jnp.int32, (length, length), 0)
    earlier = lax.broadcasted_iota(jnp.int32, (length, length), 1)
    causal = later >= earlier
    cumulative = jnp.cumsum(log_decay, axis=1)
    log_total = cumulative[:, -1]
    fall = jnp.exp(log_total[:, None] - cumulative).T
    keyed = (k.astype(F32) * fall[..., None]).astype(BF)
    update = jnp.einsum("shd,she->hde", keyed, v, preferred_element_type=F32)
    spread = cumulative[:, :, None] - cumulative[:, None, :]
    grid = jnp.where(causal, jnp.exp(jnp.where(causal, spread, 0.0)), 0.0)
    scores = jnp.einsum("thd,shd->hts", q, k, preferred_element_type=F32)
    weights = (scores * (grid * (1.0 / HEAD_DIM))).astype(BF)
    within = jnp.einsum("hts,shd->thd", weights, v, preferred_element_type=F32)
    return cumulative, log_total, update, within, q


def shards(
    queries, key_rows, values, log_decay, residual, w_out, w_gate, w_up, w_down, routes, gate_values
):
    length = queries.shape[0]
    heads = log_decay.shape[0]
    place, own = lax.axis_index("seq"), lax.axis_index("ep")
    z, y = place // SIDE, place % SIDE
    x, c = own // CORES, own % CORES
    pos_a = jnp.where(c == 0, y, z)
    pos_b = jnp.where(c == 0, z, y)

    w1, w3 = shift(w_out, "a", -1, "pair_1"), shift(w_out, "a", 1, "pair_3")

    cumulative, log_total, update, within, q = local_attention(
        queries, key_rows, values, log_decay
    )
    state, messages, w_top, w_far = entering_state(
        log_total, update, z, y, jnp.stack([w_out, w1]), w_out
    )
    w_bottom = jnp.stack([shift(w_far, "a", 2, "pair_2"), w3])
    g0, g1, g2, g3 = gather_halves(w_top, w_bottom, "b", messages)
    readout = jnp.einsum(
        "thd,hde->the", q.astype(F32), state, precision=lax.Precision.HIGHEST
    )
    carried = jnp.exp(cumulative).T[..., None] * readout * (1.0 / HEAD_DIM)
    attention = (within + carried).astype(BF).reshape(length, heads * HEAD_DIM)

    experts = lax.axis_size("ep")
    capacity = length * 9 // (4 * experts)
    steps = jnp.arange(experts, dtype=jnp.int32)
    slots = jnp.arange(capacity, dtype=jnp.int32)

    def places(ids):
        named = routes[None, :, :] == ids[:, None, None]
        is_named = jnp.any(named, axis=2)
        rank = jnp.cumsum(is_named.astype(jnp.int32), axis=1) - 1
        chosen = is_named[:, None, :] & (rank[:, None, :] == slots[None, :, None])
        return chosen, jnp.sum(jnp.where(named, gate_values[None], 0.0), axis=2)

    chosen, weight = places(steps)
    picks = places((x + steps % SIDE) % SIDE * CORES + (c + steps // SIDE) % CORES)[0].astype(BF)
    attention, picks = lax.optimization_barrier((attention, picks))

    def table(offsets):
        a = (pos_a + jnp.array([o[0] for o in offsets])) % SIDE
        b = (pos_b + jnp.array([o[1] for o in offsets])) % SIDE
        j = jnp.where(c == 0, b * SIDE + a, a * SIDE + b)
        e = j // 2
        return ((((e % 2) != c) * SIDE + (e // 2 - x) % SIDE) * 2 + j % 2).astype(jnp.int32)

    everyone = lambda *bs: table([(a, b) for b in bs for a in range(SIDE)])
    partial = project(attention, g0, everyone(0), None)
    partial = project(attention, g1 + g3, everyone(1, 3), partial)
    partial = project(attention, g2, everyone(2), partial)

    other = send(partial[1], lambda pz, py, px, pc: (pz, py, px, pc + 1))
    both = [add(partial[0][d], other[d]) for d in range(SIDE)]
    arrived = [
        send(both[d].astype(BF), functools.partial(lambda d, pz, py, px, pc: (pz, py, px + d, pc), d))
        for d in range(1, SIDE)
    ]
    stream = add(residual, both[0], *arrived).astype(BF)

    width = stream.shape[1]
    wide = stream.astype(F32)
    squares = jnp.sum(wide * wide, axis=1, keepdims=True)
    s0 = squares.astype(BF).astype(F32)
    s1 = (squares - s0).astype(BF).astype(F32)
    s2 = squares - s0 - s1
    lane = lax.broadcasted_iota(jnp.int32, (length, 128), 1)
    tail = jnp.where(lane == 0, s0, jnp.where(lane == 1, s1, jnp.where(lane == 2, s2, 0.0)))
    rows = jnp.concatenate([stream, tail.astype(BF)], axis=1)
    picked = jnp.dot(
        picks.reshape(experts * capacity, length), rows, preferred_element_type=F32
    ).astype(BF)
    picked = picked.reshape(experts, capacity, width + 128)
    got = jnp.stack(exchange([picked[k] for k in range(experts)]))
    square_sum = jnp.sum(got[:, :, width : width + 3].astype(F32), axis=(0, 2))
    scale = lax.rsqrt(square_sum / (experts * width) + EPSILON)
    place_of = (steps - c) % CORES * SIDE + (x - steps // CORES) % SIDE
    normed = (got[:, :, :width].astype(F32) * scale[None, :, None]).astype(BF)
    packed = jnp.transpose(normed[place_of], (1, 0, 2)).reshape(capacity, experts * width)

    half = packed.shape[1] // 2
    c1, c3 = shift(packed, "a", -1, "pair_1"), shift(packed, "a", 1, "pair_3")
    halves = lambda m, n: [
        jnp.concatenate([p[:, i * half : (i + 1) * half] for p in (m, n)], axis=0) for i in range(2)
    ]
    odd_l, odd_r, _ = ring_rows(*halves(c1, c3), "odd")
    c2l = shift(c1[:, :half], "a", -1, "pair_2_left")
    c2r = shift(c3[:, half:], "a", 1, "pair_2_right")
    even_own = [
        jnp.concatenate([packed[:, :half], c2l], axis=0),
        jnp.concatenate([packed[:, half:], c2r], axis=0),
    ]
    even_own, _ = lax.optimization_barrier((even_own, (odd_l[1], odd_r[3])))
    gate_rows, up_rows, down = w_gate[0].T, w_up[0].T, w_down[0]
    hidden_odd = lift(odd_l, odd_r, gate_rows, up_rows)
    even_l, even_r, hidden_odd = ring_rows(*even_own, "even", hidden_odd)
    hidden_even = lift(even_l, even_r, gate_rows, up_rows)
    part_l, part_r = (lower(hidden_odd, down, SIDE, side) for side in range(2))
    sum_odd_l, sum_odd_r, hidden_even = ring_sums(part_l, part_r, "back_odd", hidden_even)
    part_l, part_r = (lower(hidden_even, down, SIDE, side) for side in range(2))
    sum_even_l, sum_even_r, _ = ring_sums(part_l, part_r, "back_even")
    mine = []
    for odd, even, n in ((sum_odd_l, sum_even_l, "left"), (sum_odd_r, sum_even_r, "right")):
        mine.append(
            add(
                even[:capacity],
                shift(even[capacity:].astype(BF), "a", 2, "back_pair_2_" + n),
                shift(odd[:capacity].astype(BF), "a", 1, "back_pair_1_" + n),
                shift(odd[capacity:].astype(BF), "a", -1, "back_pair_3_" + n),
            ).astype(BF)
        )

    returned = lax.all_to_all(
        jnp.concatenate(
            [jnp.transpose(m.reshape(capacity, experts // 2, width), (1, 0, 2)) for m in mine], axis=0
        ),
        "ep",
        0,
        0,
    )
    w_hi = weight.astype(BF).astype(F32)
    w_lo = weight - w_hi
    spread = jnp.concatenate(
        [jnp.where(chosen, w[:, None, :], 0.0).astype(BF) for w in (w_hi, w_lo)], axis=0
    ).reshape(2 * experts * capacity, length)
    flat = returned.reshape(experts * capacity, width)
    mix = lax.dot_general(
        spread,
        jnp.concatenate([flat, flat], axis=0),
        (((0,), (0,)), ((), ())),
        preferred_element_type=F32,
    )
    return attention, mix.astype(BF)


def solution(mesh):
    placed = (
        P("seq", "ep"),
        P("seq", "ep"),
        P("seq", "ep"),
        P("ep", "seq"),
        P("seq", "ep"),
        P("ep", "seq"),
        P("ep", None, "seq"),
        P("ep", None, "seq"),
        P("ep", "seq", None),
        P("seq", None),
        P("seq", None),
    )
    return jax.shard_map(
        shards,
        mesh=mesh,
        in_specs=placed,
        out_specs=(P("seq", "ep"), P("seq", "ep")),
        check_vma=False,
    )
```
